32 devices in a mesh: comp: 2 (over core), rank: 16 (over z, y, x).
Axes of the slice: x: 2, y: 2, z: 4, core: 2. Of those that a mesh axis runs over, the one named last changes fastest.
Arguments:
- surface_fields: bfloat16 [2, 40, 65536], P('comp', None, 'rank'), may hold values from -6 to 6
- cell_area: float32 [2, 65536], P('comp', 'rank'), may hold values from 0.5 to 2
- remap_tiles: bfloat16 [2048, 128, 128], P('rank'), may hold values from -0.5 to 0.5
- pair_blocks: int32 [16, 16], P('rank'), may hold values from 0 to 8, as said below
- slot_cell: int32 [16, 16, 8], P('rank'), may hold values from 0 to 31
- node_block: int32 [16, 128], P('rank'), may hold values from 0 to 31
Outputs:
- surface_fluxes: float32 [2, 20, 65536], P('comp', None, 'rank')
The draws below stay inside these ranges and needn't reach their ends.
Inputs may be any that keep to these rules, and one draw needn't show every extreme that they name: `pair_blocks`: entry [q, d] counts the live slots from atmosphere rank q to ocean rank d; in some rank's row every entry is 8.
All inputs are finite; a program needn't handle non-finite values.
Results may differ from the reference program's by a relative error of at most 0.0036.
Values may be sent and summed in bfloat16 or wider, within the bound.
No kernel may reach another device: no remote copies, remote signals or barrier semaphores. Data moves between devices by JAX's collectives and lax.ppermute only.
A program may use at most 128 MiB of HBM per device.

```python
import math
import jax
import jax.numpy as jnp
from jax import lax

F_A = 40
F_F = 20
BS = 128
FLUX_IT = 5
NCB = 32
SLOTS = 8
NB = 128
NODES = 65536
N_RANK = 16


def draw_pair_blocks(key, part):
    key_level, key_busy, key_place = jax.random.split(key, 3)
    level = jax.random.randint(key_level, (N_RANK,), 0, 4)
    busiest = jax.random.randint(key_busy, (), 0, N_RANK)
    level = jnp.where(jnp.arange(N_RANK) == busiest, 3, level)
    factor = jnp.array([1, 2, 4, 8], jnp.int32)[level]
    live_total = SLOTS * N_RANK // 8 * factor
    position = jax.vmap(lambda subkey: jax.random.permutation(subkey, N_RANK))(jax.random.split(key_place, N_RANK))
    counts = (live_total[:, None] - position + N_RANK - 1) // N_RANK
    return jnp.clip(counts, 0, SLOTS).astype(jnp.int32)


def set_ends(values, stream_key, least, largest):
    longest = values.shape.index(max(values.shape))
    spots = []
    for shift in (0, 1):
        where = [jax.random.randint(jax.random.fold_in(stream_key, axis), (), 0, length) for axis, length in enumerate(values.shape)]
        where[longest] = (where[longest] + shift) % values.shape[longest]
        spots.append(tuple(where))
    return values.at[spots[0]].set(least).at[spots[1]].set(largest)


def block_levels(own_key, extent, cuts, low, largest):
    def one(dim, blocks):
        draws = jax.random.uniform(jax.random.fold_in(jax.random.fold_in(own_key, 6), dim), (blocks,), jnp.float32, low / len(cuts), largest / len(cuts))
        return jnp.repeat(jnp.exp(draws), extent[dim] // blocks).reshape((-1,) + (1,) * (len(extent) - dim - 1))

    level = one(*cuts[0])
    for cut in cuts[1:]:
        level = level * one(*cut)
    return level


def gaussian(own_key, dims, scale, most, cuts=(), held_as=jnp.bfloat16):
    gain = block_levels(own_key, dims, cuts, -0.22, 0.18) if cuts else 1.0
    entries = jax.random.normal(own_key, dims, jnp.float32) * scale * gain
    return jnp.minimum(jnp.maximum(entries, -most), most).astype(held_as)


def setup_inputs(seed: int = 0) -> dict:
    streams_of = jax.random.split(jax.random.key(seed), 7)
    surface_fields = gaussian(streams_of[0], (2, F_A, NODES), 1.0, 6.0, ((0, 2), (2, 16)))
    cell_area = jnp.clip(jnp.exp(math.log(2.0) - 1.3862944 * jax.random.uniform(streams_of[1], (2, NODES), jnp.float32) ** block_levels(streams_of[1], (2, NODES), ((0, 2), (1, 16)), -0.2, 0.2)), 0.5, 2.0)
    remap_tiles = gaussian(streams_of[2], (N_RANK * NB, BS, BS), BS ** -0.5, 0.5, ((0, 16),))
    pair_blocks = draw_pair_blocks(jax.random.fold_in(streams_of[6], 71), 0)
    slot_cell = set_ends(jax.random.randint(streams_of[4], (N_RANK, N_RANK, SLOTS), 0, NCB), jax.random.fold_in(streams_of[4], 1), 0, NCB - 1).astype(jnp.int32)
    node_block = set_ends(jax.random.randint(streams_of[5], (N_RANK, NB), 0, NCB), jax.random.fold_in(streams_of[5], 1), 0, NCB - 1).astype(jnp.int32)
    return dict(surface_fields=surface_fields, cell_area=cell_area, remap_tiles=remap_tiles, pair_blocks=pair_blocks, slot_cell=slot_cell, node_block=node_block)


def reference(surface_fields, cell_area, remap_tiles, pair_blocks, slot_cell, node_block):
    slot_total = SLOTS * N_RANK
    atmosphere = surface_fields[0].reshape(F_A, N_RANK, NCB, BS)
    ocean = surface_fields[1].astype(jnp.float32).reshape(F_A, N_RANK, NCB, BS).transpose(1, 2, 0, 3)
    tile_grid = remap_tiles.reshape(N_RANK, slot_total, BS, BS)
    live_mask = (jnp.arange(SLOTS)[None, None, :] < pair_blocks[:, :, None]).astype(jnp.float32).reshape(N_RANK, slot_total)
    dest_rank = jnp.repeat(jnp.arange(N_RANK, dtype=jnp.int32), SLOTS)
    slot_index = jnp.tile(jnp.arange(SLOTS, dtype=jnp.int32), N_RANK)

    def forward(carry, source_rank):
        blocks = jnp.take(atmosphere[:, source_rank], node_block[source_rank], axis=1)
        contrib = jnp.einsum('fjn,jnc->jfc', blocks.astype(jnp.float32), tile_grid[source_rank].astype(jnp.float32))
        contrib = contrib * live_mask[source_rank][:, None, None]
        contrib = lax.optimization_barrier(contrib.astype(jnp.bfloat16)).astype(jnp.float32)
        cell_index = slot_cell[dest_rank, source_rank, slot_index]
        return (carry.at[dest_rank, cell_index].add(contrib), None)
    start = jnp.zeros((N_RANK, NCB, F_A, BS), jnp.float32)
    remapped = lax.scan(forward, start, jnp.arange(N_RANK, dtype=jnp.int32))[0]
    wind_u = remapped[:, :, 0] - ocean[:, :, 0]
    wind_v = remapped[:, :, 1] - ocean[:, :, 1]
    wind_speed = jnp.sqrt(wind_u * wind_u + wind_v * wind_v + 0.25)
    stability = 1.0 + 4.0 * jax.nn.sigmoid(remapped[:, :, 2] - ocean[:, :, 2])
    transfer = jnp.ones_like(wind_speed)
    for sweep in range(FLUX_IT):
        transfer = 1.0 / (1.0 + stability * transfer)
    fluxes = (transfer * wind_speed)[:, :, None] * (remapped[:, :, :F_F] - ocean[:, :, :F_F]) + remapped[:, :, F_F:] * ocean[:, :, F_F:]
    weighted = (fluxes * cell_area[1].reshape(N_RANK, NCB, 1, BS)).astype(jnp.bfloat16)

    def backward(carry, source_rank):
        cell_index = slot_cell[dest_rank, source_rank, slot_index]
        pieces = weighted[dest_rank, cell_index]
        contrib = jnp.einsum('jfc,jnc->jfn', pieces.astype(jnp.float32), tile_grid[source_rank].astype(jnp.float32))
        contrib = contrib * live_mask[source_rank][:, None, None]
        node_sums = jnp.zeros((NCB, F_F, BS), jnp.float32).at[node_block[source_rank]].add(contrib)
        return (carry, node_sums)
    node_sums = lax.scan(backward, jnp.zeros((), jnp.float32), jnp.arange(N_RANK, dtype=jnp.int32))[1]
    atm_flux = node_sums.transpose(2, 0, 1, 3).reshape(F_F, NODES) / cell_area[0][None, :]
    ocean_flux = fluxes.transpose(2, 0, 1, 3).reshape(F_F, NODES)
    return jnp.stack([atm_flux, ocean_flux])
```

```python
import functools

import jax
import jax.numpy as jnp
from jax import lax
from jax.experimental import pallas as pl
from jax.experimental.pallas import tpu as pltpu
from jax.sharding import PartitionSpec as P

FLUX_IT = 5
DEVICES = ("comp", "rank")


def swap_cores(value):
    return lax.ppermute(value, "comp", [(0, 1), (1, 0)])


def low_lanes(shape):
    return lax.broadcasted_iota(jnp.int32, shape, len(shape) - 1) < shape[-1] // 2


def forward_kernel(core, counts, node_block, fields, tiles, out):
    dests, half = tiles.shape[0], tiles.shape[2]
    field_rows, width = fields.shape[0], tiles.shape[4]
    first = pl.program_id(0) * dests
    offset = core[0] * half
    low = low_lanes((field_rows, width))
    for d in range(dests):
        live = counts[first + d]
        lows, highs = [], []
        for pair in range(half // 2):
            products = []
            for i in (2 * pair, 2 * pair + 1):
                slot = offset + i
                block = node_block[(first + d) * 2 * half + slot]
                source = fields[:, pl.ds(pl.multiple_of(block * width, width), width)]
                product = jnp.dot(source, tiles[d, 0, i], preferred_element_type=jnp.float32)
                products.append(jnp.where(slot < live, product, 0.0))
            even, odd = products
            lows.append(jnp.where(low, even, pltpu.roll(odd, width // 2, 1)))
            highs.append(jnp.where(low, pltpu.roll(even, width // 2, 1), odd))
        out[0, d] = jnp.concatenate(lows, axis=0).astype(out.dtype)
        out[1, d] = jnp.concatenate(highs, axis=0).astype(out.dtype)


def back_kernel(core, counts, node_block, pieces, tiles, out, sums):
    dests, half = tiles.shape[0], tiles.shape[2]
    rows, width = pieces.shape[2], pieces.shape[3]
    flux_rows = out.shape[0]
    step = pl.program_id(0)
    first = step * dests
    offset = core[0] * half
    low = low_lanes((rows, width))

    @pl.when(step == 0)
    def _():
        sums[...] = jnp.zeros_like(sums)

    for d in range(dests):
        live = counts[first + d]
        zero = pieces[0, d].astype(jnp.float32)
        one = pieces[1, d].astype(jnp.float32)
        whole = (
            jnp.where(low, zero, pltpu.roll(one, width // 2, 1)),
            jnp.where(low, pltpu.roll(zero, width // 2, 1), one),
        )
        for i in range(half):
            pair = i // 2
            slot = offset + i
            block = node_block[(first + d) * 2 * half + slot]
            product = lax.dot_general(
                whole[i % 2][pair * flux_rows : (pair + 1) * flux_rows].astype(jnp.bfloat16),
                tiles[d, 0, i],
                (((1,), (1,)), ((), ())),
                preferred_element_type=jnp.float32,
            )
            sums[block] += jnp.where(slot < live, product, 0.0)

    @pl.when(step == pl.num_programs(0) - 1)
    def _():
        for block in range(sums.shape[0]):
            out[:, block * width : (block + 1) * width] = sums[block]


def on_device(surface_fields, cell_area, remap_tiles, pair_blocks, slot_cell, node_block):
    rank_count = lax.axis_size("rank")
    fields = surface_fields[0]
    width = remap_tiles.shape[1]
    slot_total = remap_tiles.shape[0]
    pair_slots = slot_cell.shape[2]
    half = pair_slots // 2
    pairs = half // 2
    field_rows, points = fields.shape
    flux_rows = field_rows // 2
    nblocks = points // width
    core = lax.axis_index("comp")
    on_ocean = core == 1
    core_ref = core.astype(jnp.int32)[None]
    counts = pair_blocks[0]
    slot_nodes = node_block[0]
    tiles = remap_tiles.reshape(rank_count, 2, half, width, width)

    other_fields = swap_cores(fields)
    other_area = swap_cores(cell_area)
    atmosphere = jnp.where(on_ocean, other_fields, fields)
    ocean = jnp.where(on_ocean, fields, other_fields)
    ocean_area = jnp.where(on_ocean, cell_area, other_area)[0]

    dests = 4
    grid = (rank_count // dests,)
    tile_spec = pl.BlockSpec(
        (dests, 1, half, width, width), lambda g, core, *_: (g, core[0], 0, 0, 0)
    )
    outgoing = pl.pallas_call(
        forward_kernel,
        grid_spec=pltpu.PrefetchScalarGridSpec(
            num_scalar_prefetch=3,
            grid=grid,
            in_specs=[pl.BlockSpec((field_rows, points), lambda g, *_: (0, 0)), tile_spec],
            out_specs=pl.BlockSpec(
                (2, dests, pairs * field_rows, width), lambda g, *_: (0, g, 0, 0)
            ),
        ),
        out_shape=jax.ShapeDtypeStruct(
            (2, rank_count, pairs * field_rows, width), jnp.bfloat16
        ),
        name="forward_products",
    )(core_ref, counts, slot_nodes, atmosphere, tiles)

    arrived = lax.all_to_all(
        outgoing.reshape(2 * rank_count, pairs * field_rows, width),
        DEVICES,
        split_axis=0,
        concat_axis=0,
        tiled=True,
    )

    cells = slot_cell[0].reshape(rank_count, 2, pairs, 2).transpose(3, 1, 0, 2).reshape(2, -1)
    entries = cells.shape[1]
    block_ids = jnp.arange(nblocks, dtype=jnp.int32)
    onehot = (cells[:, None, :] == block_ids[None, :, None]).astype(jnp.bfloat16)
    both = jnp.einsum(
        "ck,kfb->cfb",
        onehot.reshape(2 * nblocks, entries),
        arrived.reshape(entries, field_rows, width),
        preferred_element_type=jnp.float32,
    )
    mid = width // 2
    remapped = both[:nblocks, :, :mid] + both[nblocks:, :, mid:]
    surface = ocean.reshape(field_rows, nblocks, 2, mid)
    surface = jnp.where(on_ocean, surface[:, :, 1], surface[:, :, 0])
    surface = surface.transpose(1, 0, 2).astype(jnp.float32)
    area = ocean_area.reshape(nblocks, 2, mid)
    area = jnp.where(on_ocean, area[:, 1], area[:, 0])
    wind_u = remapped[:, 0] - surface[:, 0]
    wind_v = remapped[:, 1] - surface[:, 1]
    wind_speed = jnp.sqrt(wind_u * wind_u + wind_v * wind_v + 0.25)
    stability = 1.0 + 4.0 * jax.nn.sigmoid(remapped[:, 2] - surface[:, 2])
    transfer = jnp.ones_like(wind_speed)
    for sweep in range(FLUX_IT):
        transfer = 1.0 / (1.0 + stability * transfer)
    fluxes = (transfer * wind_speed)[:, None, :] * (
        remapped[:, :flux_rows] - surface[:, :flux_rows]
    ) + remapped[:, flux_rows:] * surface[:, flux_rows:]
    weighted = (fluxes * area[:, None, :]).astype(jnp.bfloat16)
    half_flux = fluxes.transpose(1, 0, 2)
    ocean_flux = jnp.stack(
        [jnp.where(on_ocean, 0.0, half_flux), jnp.where(on_ocean, half_flux, 0.0)], axis=2
    ).reshape(flux_rows, points)

    picks = jnp.einsum(
        "eck,cfb->ekfb", onehot, weighted, preferred_element_type=jnp.float32
    ).astype(jnp.bfloat16)
    sending = jnp.concatenate([picks[0], picks[1]], axis=-1)
    returned = lax.all_to_all(
        sending.reshape(2 * rank_count, pairs * flux_rows, width),
        DEVICES,
        split_axis=0,
        concat_axis=0,
        tiled=True,
    )

    node_sums = pl.pallas_call(
        back_kernel,
        grid_spec=pltpu.PrefetchScalarGridSpec(
            num_scalar_prefetch=3,
            grid=grid,
            in_specs=[
                pl.BlockSpec((2, dests, pairs * flux_rows, width), lambda g, *_: (0, g, 0, 0)),
                tile_spec,
            ],
            out_specs=pl.BlockSpec((flux_rows, points), lambda g, *_: (0, 0)),
            scratch_shapes=[pltpu.VMEM((nblocks, flux_rows, width), jnp.float32)],
        ),
        out_shape=jax.ShapeDtypeStruct((flux_rows, points), jnp.float32),
        name="node_sums",
    )(
        core_ref,
        counts,
        slot_nodes,
        returned.reshape(2, rank_count, pairs * flux_rows, width),
        tiles,
    )

    other = swap_cores(jnp.where(on_ocean, node_sums, ocean_flux))
    atm_flux = (node_sums + other) / cell_area
    return jnp.where(on_ocean, ocean_flux + other, atm_flux)[None]


def solution(mesh):
    return jax.shard_map(
        on_device,
        mesh=mesh,
        in_specs=(
            P("comp", None, "rank"),
            P("comp", "rank"),
            P("rank", None, None),
            P("rank", None),
            P("rank", None, None),
            P("rank", None),
        ),
        out_specs=P("comp", None, "rank"),
        check_vma=False,
    )
```

```python
import functools

import jax
import jax.numpy as jnp
from jax import lax
from jax.experimental import pallas as pl
from jax.experimental.pallas import tpu as pltpu
from jax.sharding import PartitionSpec as P

FLUX_IT = 5
DEVICES = ("comp", "rank")
SMEM = pl.BlockSpec(memory_space=pltpu.SMEM)
VMEM = pl.BlockSpec(memory_space=pltpu.VMEM)
ANY = pl.BlockSpec(memory_space=pl.ANY)
PARAMS = pltpu.CompilerParams(vmem_limit_bytes=40 << 20)


def swap_cores(value):
    return lax.ppermute(value, "comp", [(0, 1), (1, 0)])


def low_lanes(shape):
    return lax.broadcasted_iota(jnp.int32, shape, len(shape) - 1) < shape[-1] // 2


def half_turn(value):
    return pltpu.roll(value, value.shape[-1] // 2, value.ndim - 1)


def load_kernel(core, tiles, out, sem):
    copy = pltpu.make_async_copy(tiles.at[:, core[0]], out, sem)
    copy.start()
    copy.wait()


def forward_kernel(core, counts, node_block, mine, other, tiles, out, fields, packed, sems):
    rank_count, half, _, width = tiles.shape
    field_rows = fields.shape[0]
    offset = core[0] * half
    low = low_lanes((field_rows, width))
    parts = sems.shape[0]
    step = rank_count // parts

    @pl.when(core[0] == 0)
    def _():
        fields[...] = mine[...]

    @pl.when(core[0] == 1)
    def _():
        fields[...] = other[...]

    copies = []
    for part in range(parts):
        for d in range(part * step, (part + 1) * step):
            live = counts[d]
            lows, highs = [], []
            for pair in range(half // 2):
                products = []
                for i in (2 * pair, 2 * pair + 1):
                    block = node_block[d * 2 * half + offset + i]
                    source = fields[:, pl.ds(pl.multiple_of(block * width, width), width)]
                    product = jnp.dot(source, tiles[d, i], preferred_element_type=jnp.float32)
                    products.append(jnp.where(offset + i < live, product, 0.0))
                even, odd = products
                lows.append(jnp.where(low, even, half_turn(odd)))
                highs.append(jnp.where(low, half_turn(even), odd))
            packed[0, d] = jnp.concatenate(lows, axis=0).astype(packed.dtype)
            packed[1, d] = jnp.concatenate(highs, axis=0).astype(packed.dtype)
        ready = pl.ds(part * step, step)
        copies.append(pltpu.make_async_copy(packed.at[:, ready], out.at[:, ready], sems.at[part]))
        copies[-1].start()
    for copy in copies:
        copy.wait()


def ocean_kernel(core, slot_cell, sums, surface, area, sending, flux, weighted):
    field_rows, nblocks, width = surface.shape
    flux_rows = field_rows // 2
    rank_count, pair_slots = slot_cell.shape
    half = pair_slots // 2
    low = low_lanes((nblocks, width))
    own = low == (core[0] == 0)

    def remapped(k):
        mixed = jnp.where(low, sums[k, :nblocks], sums[k, nblocks:])
        return mixed + half_turn(mixed)

    wind_u = remapped(0) - surface[0]
    wind_v = remapped(1) - surface[1]
    wind_speed = jnp.sqrt(wind_u * wind_u + wind_v * wind_v + 0.25)
    stability = 1.0 + 4.0 * jax.nn.sigmoid(remapped(2) - surface[2])
    transfer = jnp.ones_like(wind_speed)
    for sweep in range(FLUX_IT):
        transfer = 1.0 / (1.0 + stability * transfer)
    exchange = transfer * wind_speed
    for k in range(flux_rows):
        value = exchange * (remapped(k) - surface[k]) + remapped(k + flux_rows) * surface[
            k + flux_rows
        ]
        flux[k] = jnp.where(own, value, 0.0)
        weighted[:, k, :] = value * area[...]

    low = low_lanes((flux_rows, width))
    for source in range(rank_count):
        for part in range(2):
            rows = []
            for pair in range(half // 2):
                even = slot_cell[source, part * half + 2 * pair]
                odd = slot_cell[source, part * half + 2 * pair + 1]
                rows.append(jnp.where(low, weighted[even], weighted[odd]))
            sending[part, source] = jnp.concatenate(rows, axis=0).astype(sending.dtype)


def back_kernel(core, counts, node_block, pieces, tiles, out, sums):
    rank_count, half, _, width = tiles.shape
    rows = pieces.shape[2]
    flux_rows = out.shape[0]
    offset = core[0] * half
    low = low_lanes((rows, width))
    sums[...] = jnp.zeros_like(sums)
    for d in range(rank_count):
        live = counts[d]
        zero = pieces[0, d].astype(jnp.float32)
        one = pieces[1, d].astype(jnp.float32)
        whole = (jnp.where(low, zero, half_turn(one)), jnp.where(low, half_turn(zero), one))
        for i in range(half):
            pair = i // 2
            block = node_block[d * 2 * half + offset + i]
            product = lax.dot_general(
                whole[i % 2][pair * flux_rows : (pair + 1) * flux_rows].astype(jnp.bfloat16),
                tiles[d, i],
                (((1,), (1,)), ((), ())),
                preferred_element_type=jnp.float32,
            )
            sums[block] += jnp.where(offset + i < live, product, 0.0)
    for k in range(flux_rows):
        out[k] = sums[:, k, :]


def on_device(surface_fields, cell_area, remap_tiles, pair_blocks, slot_cell, node_block):
    rank_count = lax.axis_size("rank")
    fields = surface_fields[0]
    width = remap_tiles.shape[1]
    pair_slots = slot_cell.shape[2]
    half = pair_slots // 2
    pairs = half // 2
    field_rows, points = fields.shape
    flux_rows = field_rows // 2
    nblocks = points // width
    core = lax.axis_index("comp")
    on_ocean = core == 1
    core_ref = core.astype(jnp.int32)[None]
    counts = pair_blocks[0]
    slot_nodes = node_block[0]

    other_fields = swap_cores(fields)
    other_area = swap_cores(cell_area)

    tiles = pl.pallas_call(
        load_kernel,
        in_specs=[SMEM, ANY],
        out_specs=VMEM,
        out_shape=pltpu.VMEM((rank_count, half, width, width), jnp.bfloat16),
        scratch_shapes=[pltpu.SemaphoreType.DMA],
        compiler_params=PARAMS,
        name="load_tiles",
    )(core_ref, remap_tiles.reshape(rank_count, 2, half, width, width))

    parts = 4
    message = (2, rank_count, pairs * field_rows, width)
    outgoing = pl.pallas_call(
        forward_kernel,
        in_specs=[SMEM, SMEM, SMEM, VMEM, VMEM, VMEM],
        out_specs=ANY,
        out_shape=jax.ShapeDtypeStruct(message, jnp.bfloat16),
        scratch_shapes=[
            pltpu.VMEM(fields.shape, jnp.bfloat16),
            pltpu.VMEM(message, jnp.bfloat16),
            pltpu.SemaphoreType.DMA((parts,)),
        ],
        compiler_params=PARAMS,
        name="forward_products",
    )(core_ref, counts, slot_nodes, fields, other_fields, tiles)

    arrived = lax.all_to_all(
        outgoing.reshape(2 * rank_count, pairs * field_rows, width),
        DEVICES,
        split_axis=0,
        concat_axis=0,
        tiled=True,
    )

    def own_columns(values, other):
        values = jnp.where(on_ocean, values, other).reshape(-1, nblocks, 2, width // 2)
        values = jnp.where(on_ocean, values[:, :, 1], values[:, :, 0]).astype(jnp.float32)
        return jnp.concatenate([values, values], axis=-1)

    surface = own_columns(fields, other_fields)
    area = own_columns(cell_area, other_area)[0]

    cells = slot_cell[0].reshape(rank_count, 2, pairs, 2).transpose(3, 1, 0, 2).reshape(2, -1)
    entries = cells.shape[1]
    block_ids = jnp.arange(nblocks, dtype=jnp.int32)
    onehot = (cells[:, None, :] == block_ids[None, :, None]).astype(jnp.bfloat16)
    sums = jnp.einsum(
        "ck,kfb->fcb",
        onehot.reshape(2 * nblocks, entries),
        arrived.reshape(entries, field_rows, width),
        preferred_element_type=jnp.float32,
    )
    sending, ocean_flux = pl.pallas_call(
        ocean_kernel,
        in_specs=[SMEM, SMEM, VMEM, VMEM, VMEM],
        out_specs=[VMEM, VMEM],
        out_shape=[
            jax.ShapeDtypeStruct((2, rank_count, pairs * flux_rows, width), jnp.bfloat16),
            jax.ShapeDtypeStruct((flux_rows, nblocks, width), jnp.float32),
        ],
        scratch_shapes=[pltpu.VMEM((nblocks, flux_rows, width), jnp.float32)],
        compiler_params=PARAMS,
        name="ocean_fluxes",
    )(core_ref, slot_cell[0], sums, surface, area)
    other_flux = swap_cores(ocean_flux)

    returned = lax.all_to_all(
        sending.reshape(2 * rank_count, pairs * flux_rows, width),
        DEVICES,
        split_axis=0,
        concat_axis=0,
        tiled=True,
    )

    node_sums = pl.pallas_call(
        back_kernel,
        in_specs=[SMEM, SMEM, SMEM, VMEM, VMEM],
        out_specs=VMEM,
        out_shape=jax.ShapeDtypeStruct((flux_rows, nblocks, width), jnp.float32),
        scratch_shapes=[pltpu.VMEM((nblocks, flux_rows, width), jnp.float32)],
        compiler_params=PARAMS,
        name="node_sums",
    )(
        core_ref,
        counts,
        slot_nodes,
        returned.reshape(2, rank_count, pairs * flux_rows, width),
        tiles,
    )

    other_sums = swap_cores(node_sums)
    atm_flux = (node_sums + other_sums) / cell_area.reshape(nblocks, width)
    result = jnp.where(on_ocean, ocean_flux + other_flux, atm_flux)
    return result.reshape(1, flux_rows, points)


def solution(mesh):
    return jax.shard_map(
        on_device,
        mesh=mesh,
        in_specs=(
            P("comp", None, "rank"),
            P("comp", "rank"),
            P("rank", None, None),
            P("rank", None),
            P("rank", None, None),
            P("rank", None),
        ),
        out_specs=P("comp", None, "rank"),
        check_vma=False,
    )
```

```python
import jax
import jax.numpy as jnp
from jax import lax
from jax.experimental import pallas as pl
from jax.experimental.pallas import tpu as pltpu
from jax.sharding import PartitionSpec as P

FLUX_IT = 5
DEVICES = ("comp", "rank")
SMEM = pl.BlockSpec(memory_space=pltpu.SMEM)
VMEM = pl.BlockSpec(memory_space=pltpu.VMEM)
ANY = pl.BlockSpec(memory_space=pl.ANY)
PARAMS = pltpu.CompilerParams(vmem_limit_bytes=24 << 20)


def swap_cores(value):
    return lax.ppermute(value, "comp", [(0, 1), (1, 0)])


def low_lanes(shape):
    return lax.broadcasted_iota(jnp.int32, shape, len(shape) - 1) < shape[-1] // 2


def half_turn(value):
    return pltpu.roll(value, value.shape[-1] // 2, value.ndim - 1)


def load_kernel(core, tiles, out, sem):
    copy = pltpu.make_async_copy(tiles.at[:, core[0]], out, sem)
    copy.start()
    copy.wait()


def forward_kernel(core, counts, node_block, mine, other, tiles, packed, fields):
    rank_count, half, _, width = tiles.shape
    field_rows = fields.shape[0]
    offset = core[0] * half
    low = low_lanes((field_rows, width))

    @pl.when(core[0] == 0)
    def _():
        fields[...] = mine[...]

    @pl.when(core[0] == 1)
    def _():
        fields[...] = other[...]

    for d in range(rank_count):
        live = counts[d]
        lows, highs = [], []
        for pair in range(half // 2):
            first = d * 2 * half + offset + 2 * pair
            sources = [
                fields[:, pl.ds(pl.multiple_of(node_block[slot] * width, width), width)]
                for slot in (first, first + 1)
            ]
            products = jnp.dot(
                jnp.concatenate(sources, axis=0),
                jnp.concatenate([tiles[d, 2 * pair], tiles[d, 2 * pair + 1]], axis=1),
                preferred_element_type=jnp.float32,
            )
            even = jnp.where(offset + 2 * pair < live, products[:field_rows, :width], 0.0)
            odd = jnp.where(offset + 2 * pair + 1 < live, products[field_rows:, width:], 0.0)
            lows.append(jnp.where(low, even, half_turn(odd)))
            highs.append(jnp.where(low, half_turn(even), odd))
        packed[d] = jnp.concatenate(lows, axis=0).astype(packed.dtype)
        packed[rank_count + d] = jnp.concatenate(highs, axis=0).astype(packed.dtype)


def ocean_kernel(
    core,
    slot_cell,
    arrived,
    mine,
    other,
    own_area,
    other_area,
    sending,
    flux,
    even_sums,
    odd_sums,
    near,
    far,
    pull,
):
    nblocks, field_rows, width = even_sums.shape
    flux_rows = field_rows // 2
    pair_slots, rank_count = slot_cell.shape
    half = pair_slots // 2
    ocean_core = core[0] == 1

    even_sums[...] = jnp.zeros_like(even_sums)
    odd_sums[...] = jnp.zeros_like(odd_sums)
    for source in range(rank_count):
        for part in range(2):
            entry = arrived[part * rank_count + source].astype(jnp.float32)
            for pair in range(half // 2):
                rows = entry[pair * field_rows : (pair + 1) * field_rows]
                slot = part * half + 2 * pair
                even_sums[slot_cell[slot, source]] += rows
                odd_sums[slot_cell[slot + 1, source]] += rows

    low = low_lanes((field_rows, width))
    own = low != ocean_core
    for block in range(nblocks):
        columns = slice(block * width, (block + 1) * width)
        mixed = jnp.where(low, even_sums[block], odd_sums[block])
        remapped = mixed + half_turn(mixed)
        surface = jnp.where(ocean_core, mine[:, columns], other[:, columns]).astype(jnp.float32)
        surface = jnp.where(own, surface, half_turn(surface))
        near[block] = remapped[:flux_rows] - surface[:flux_rows]
        far[block] = remapped[flux_rows:] * surface[flux_rows:]

    wind_u, wind_v, excess = near[:, 0, :], near[:, 1, :], near[:, 2, :]
    wind_speed = jnp.sqrt(wind_u * wind_u + wind_v * wind_v + 0.25)
    stability = 1.0 + 4.0 * jax.nn.sigmoid(excess)
    transfer = jnp.ones_like(wind_speed)
    for sweep in range(FLUX_IT):
        transfer = 1.0 / (1.0 + stability * transfer)
    pull[...] = transfer * wind_speed

    own = own[:flux_rows]
    own_rows = low_lanes((nblocks, width)) != ocean_core
    area = jnp.where(ocean_core, own_area[...], other_area[...])
    area = jnp.where(own_rows, area, half_turn(area))
    for block in range(nblocks):
        value = pull[block : block + 1] * near[block] + far[block]
        flux[:, block, :] = jnp.where(own, value, 0.0)
        far[block] = value * area[block : block + 1]

    low = low[:flux_rows]
    for source in range(rank_count):
        for part in range(2):
            rows = []
            for pair in range(half // 2):
                slot = part * half + 2 * pair
                even, odd = slot_cell[slot, source], slot_cell[slot + 1, source]
                rows.append(jnp.where(low, far[even], far[odd]))
            sending[part * rank_count + source] = jnp.concatenate(rows, axis=0).astype(
                sending.dtype
            )


def back_kernel(core, counts, node_block, pieces, tiles, flux, keep, give, sums):
    rank_count, half, _, width = tiles.shape
    rows = pieces.shape[1]
    flux_rows = flux.shape[0]
    offset = core[0] * half
    low = low_lanes((rows, width))
    sums[...] = jnp.zeros_like(sums)
    for d in range(rank_count):
        live = counts[d]
        zero = pieces[d].astype(jnp.float32)
        one = pieces[rank_count + d].astype(jnp.float32)
        whole = (jnp.where(low, zero, half_turn(one)), jnp.where(low, half_turn(zero), one))
        for i in range(half):
            pair = i // 2
            block = node_block[d * 2 * half + offset + i]
            product = lax.dot_general(
                whole[i % 2][pair * flux_rows : (pair + 1) * flux_rows].astype(jnp.bfloat16),
                tiles[d, i],
                (((1,), (1,)), ((), ())),
                preferred_element_type=jnp.float32,
            )
            sums[block] += jnp.where(offset + i < live, product, 0.0)
    atmosphere_core = core[0] == 0
    for k in range(flux_rows):
        nodes, cells = sums[:, k, :], flux[k]
        keep[k] = jnp.where(atmosphere_core, nodes, cells)
        give[k] = jnp.where(atmosphere_core, cells, nodes)


def on_device(surface_fields, cell_area, remap_tiles, pair_blocks, slot_cell, node_block):
    rank_count = lax.axis_size("rank")
    fields = surface_fields[0]
    width = remap_tiles.shape[1]
    pair_slots = slot_cell.shape[2]
    half = pair_slots // 2
    pairs = half // 2
    field_rows, points = fields.shape
    flux_rows = field_rows // 2
    nblocks = points // width
    core = lax.axis_index("comp")
    on_ocean = core == 1
    core_ref = core.astype(jnp.int32)[None]
    counts = pair_blocks[0]
    slot_nodes = node_block[0]

    other_fields = swap_cores(fields)
    other_area = swap_cores(cell_area)

    tiles = pl.pallas_call(
        load_kernel,
        in_specs=[SMEM, ANY],
        out_specs=VMEM,
        out_shape=pltpu.VMEM((rank_count, half, width, width), jnp.bfloat16),
        scratch_shapes=[pltpu.SemaphoreType.DMA],
        compiler_params=PARAMS,
        name="load_tiles",
    )(
        core_ref,
        pltpu.with_memory_space_constraint(
            remap_tiles.reshape(rank_count, 2, half, width, width), pltpu.HBM
        ),
    )

    def message(rows):
        return pltpu.VMEM((2 * rank_count, pairs * rows, width), jnp.bfloat16)

    def exchange(value):
        value = lax.all_to_all(value, DEVICES, split_axis=0, concat_axis=0, tiled=True)
        return pltpu.with_memory_space_constraint(value, pltpu.VMEM)

    outgoing = pl.pallas_call(
        forward_kernel,
        in_specs=[SMEM, SMEM, SMEM, VMEM, VMEM, VMEM],
        out_specs=VMEM,
        out_shape=message(field_rows),
        scratch_shapes=[pltpu.VMEM(fields.shape, jnp.bfloat16)],
        compiler_params=PARAMS,
        name="forward_products",
    )(core_ref, counts, slot_nodes, fields, other_fields, tiles)
    outgoing, other_area = lax.optimization_barrier((outgoing, other_area))
    arrived = exchange(outgoing)

    by_block = (nblocks, width)
    columns = pltpu.VMEM((nblocks, field_rows, width), jnp.float32)
    rows = pltpu.VMEM((nblocks, flux_rows, width), jnp.float32)
    by_flux = jax.ShapeDtypeStruct((flux_rows, nblocks, width), jnp.float32)
    sending, ocean_flux = pl.pallas_call(
        ocean_kernel,
        in_specs=[SMEM, SMEM] + [VMEM] * 5,
        out_specs=[VMEM, VMEM],
        out_shape=[message(flux_rows), by_flux],
        scratch_shapes=[columns, columns, rows, rows, pltpu.VMEM(by_block, jnp.float32)],
        compiler_params=PARAMS,
        name="ocean_fluxes",
    )(
        core_ref,
        slot_cell[0].T,
        arrived,
        fields,
        other_fields,
        cell_area.reshape(by_block),
        other_area.reshape(by_block),
    )
    returned = exchange(sending)

    keep, give = pl.pallas_call(
        back_kernel,
        in_specs=[SMEM, SMEM, SMEM, VMEM, VMEM, VMEM],
        out_specs=[VMEM, VMEM],
        out_shape=[by_flux, by_flux],
        scratch_shapes=[rows],
        compiler_params=PARAMS,
        name="node_sums",
    )(core_ref, counts, slot_nodes, returned, tiles, ocean_flux)

    divisor = jnp.where(on_ocean, 1.0, cell_area.reshape(by_block))
    return ((keep + swap_cores(give)) / divisor).reshape(1, flux_rows, points)


def solution(mesh):
    return jax.shard_map(
        on_device,
        mesh=mesh,
        in_specs=(
            P("comp", None, "rank"),
            P("comp", "rank"),
            P("rank", None, None),
            P("rank", None),
            P("rank", None, None),
            P("rank", None),
        ),
        out_specs=P("comp", None, "rank"),
        check_vma=False,
    )
```

```python
import math

import jax
import jax.numpy as jnp
from jax import lax
from jax.experimental import pallas as pl
from jax.experimental.pallas import tpu as pltpu
from jax.sharding import PartitionSpec as P

FLUX_IT = 5
DEVICES = ("comp", "rank")
SMEM = pl.BlockSpec(memory_space=pltpu.SMEM)
VMEM = pl.BlockSpec(memory_space=pltpu.VMEM)
ANY = pl.BlockSpec(memory_space=pl.ANY)
PARAMS = pltpu.CompilerParams(vmem_limit_bytes=24 << 20)


def swap_cores(value):
    return lax.ppermute(value, "comp", [(0, 1), (1, 0)])


def low_lanes(shape):
    return lax.broadcasted_iota(jnp.int32, shape, len(shape) - 1) < shape[-1] // 2


def half_turn(value):
    return pltpu.roll(value, value.shape[-1] // 2, value.ndim - 1)


def load_kernel(tiles, out, sem):
    copy = pltpu.make_async_copy(tiles, out, sem)
    copy.start()
    copy.wait()


def step_of(index, digit):
    return -index % digit


def peer_of(place, first, second, digit):
    return place[1] ^ jnp.where(place[0] == 0, first + digit * second, digit * first + second)


def forward_kernel(place, counts, node_block, mine, other, tiles, *refs):
    *messages, fields = refs
    digit = len(messages)
    field_rows, width = fields.shape[0], tiles.shape[2]
    pair_slots = tiles.shape[0] // digit**2
    low = low_lanes((field_rows, width))
    own = low == (place[0] == 0)

    @pl.when(place[0] == 0)
    def _():
        fields[...] = mine[...]

    @pl.when(place[0] == 1)
    def _():
        fields[...] = other[...]

    for index in reversed(range(digit)):
        for second in range(digit):
            peer = peer_of(place, step_of(index, digit), second, digit)
            live = counts[peer]
            rows = []
            for slot in range(0, pair_slots, 2):
                at = peer * pair_slots + slot
                sources = [
                    fields[:, pl.ds(pl.multiple_of(node_block[at + i] * width, width), width)]
                    for i in range(2)
                ]
                products = jnp.dot(
                    jnp.concatenate(sources, axis=0),
                    jnp.concatenate([tiles[at], tiles[at + 1]], axis=1),
                    preferred_element_type=jnp.float32,
                )
                even = jnp.where(slot < live, products[:field_rows, :width], 0.0)
                odd = jnp.where(slot + 1 < live, products[field_rows:, width:], 0.0)
                turned = half_turn(jnp.where(low, odd, even))
                rows.append(jnp.where(own, jnp.where(low, even, odd), turned))
            messages[index][second] = jnp.concatenate(rows, axis=0).astype(messages[0].dtype)


def repack_kernel(*refs):
    digit = (len(refs) + 1) // 2
    held, out = refs[:digit], refs[digit:]
    for index in range(1, digit):
        for first in range(digit):
            out[index - 1][first] = held[first][step_of(index, digit)]


def turn_kernel(place, tiles, out, held, sem):
    copy = pltpu.make_async_copy(tiles.at[:, place[0]], held, sem)
    copy.start()
    copy.wait()
    rank_count, sides, width, wide = out.shape
    pairs = wide // width
    for d in range(rank_count):
        for side in range(sides):
            for pair in range(pairs):
                turned = held[d, sides * pair + side].T
                out[d, side, :, pair * width : (pair + 1) * width] = turned


def add_entries(message, slot_cell, source, even_sums, odd_sums):
    field_rows = even_sums.shape[1]
    rows = message.astype(jnp.float32)
    for slot in range(0, slot_cell.shape[0], 2):
        entry = rows[slot // 2 * field_rows : (slot // 2 + 1) * field_rows]
        even_sums[slot_cell[slot, source]] += entry
        odd_sums[slot_cell[slot + 1, source]] += entry


def early_kernel(place, slot_cell, mine, other, *refs):
    *held, even_sums, odd_sums, surface = refs
    digit = len(held)
    nblocks, field_rows, width = surface.shape
    ocean_core = place[0] == 1
    own = low_lanes((field_rows, width)) != ocean_core
    even_sums[...] = jnp.zeros_like(even_sums)
    odd_sums[...] = jnp.zeros_like(odd_sums)
    for index in range(digit):
        source = peer_of(place, step_of(index, digit), 0, digit)
        add_entries(held[index][0], slot_cell, source, even_sums, odd_sums)
    for block in range(nblocks):
        columns = slice(block * width, (block + 1) * width)
        values = jnp.where(ocean_core, mine[:, columns], other[:, columns]).astype(jnp.float32)
        surface[block] = jnp.where(own, values, half_turn(values))


def ocean_kernel(place, slot_cell, surface, own_area, other_area, *refs):
    *arrived, _, _, sending, flux, even_sums, odd_sums, near, far, pull = refs
    digit = len(arrived) + 1
    nblocks, field_rows, width = surface.shape
    flux_rows = field_rows // 2
    pair_slots, rank_count = slot_cell.shape
    half = pair_slots // 2
    ocean_core = place[0] == 1

    for index in range(1, digit):
        for first in range(digit):
            source = peer_of(place, step_of(first, digit), step_of(index, digit), digit)
            add_entries(arrived[index - 1][first], slot_cell, source, even_sums, odd_sums)

    low = low_lanes((field_rows, width))
    for block in range(nblocks):
        mixed = jnp.where(low, even_sums[block], odd_sums[block])
        remapped = mixed + half_turn(mixed)
        near[block] = remapped[:flux_rows] - surface[block, :flux_rows]
        far[block] = (remapped * surface[block])[flux_rows:]

    wind_u, wind_v, excess = near[:, 0, :], near[:, 1, :], near[:, 2, :]
    wind_speed = jnp.sqrt(wind_u * wind_u + wind_v * wind_v + 0.25)
    stability = 1.0 + 4.0 * jax.nn.sigmoid(excess)
    transfer = jnp.ones_like(wind_speed)
    for sweep in range(FLUX_IT):
        transfer = 1.0 / (1.0 + stability * transfer)
    pull[...] = transfer * wind_speed

    own = low_lanes((flux_rows, width)) != ocean_core
    own_rows = low_lanes((nblocks, width)) != ocean_core
    area = jnp.where(ocean_core, own_area[...], other_area[...])
    area = jnp.where(own_rows, area, half_turn(area))
    for block in range(nblocks):
        value = pull[block : block + 1] * near[block] + far[block]
        flux[:, block, :] = jnp.where(own, value, 0.0)
        far[block] = value * area[block : block + 1]

    low = low[:flux_rows]
    for source in range(rank_count):
        for part in range(2):
            rows = []
            for pair in range(half // 2):
                slot = part * half + 2 * pair
                even, odd = slot_cell[slot, source], slot_cell[slot + 1, source]
                rows.append(jnp.where(low, far[even], far[odd]))
            sending[part * rank_count + source] = jnp.concatenate(rows, axis=0).astype(
                sending.dtype
            )


def back_kernel(place, counts, node_block, pieces, turned, flux, keep, give, *sums):
    rank_count, sides, width, _ = turned.shape
    rows = pieces.shape[1]
    flux_rows, nblocks, _ = flux.shape
    pairs = rows // flux_rows
    half = sides * pairs
    span = sums[0].shape[1]
    starts = [pair * flux_rows // 8 * 8 for pair in range(pairs)]
    low = low_lanes((rows, width))
    for total in sums:
        total[...] = jnp.zeros_like(total)
    for d in range(rank_count):
        live = counts[d]
        zero = pieces[d].astype(jnp.float32)
        one = pieces[rank_count + d].astype(jnp.float32)
        whole = (jnp.where(low, zero, half_turn(one)), jnp.where(low, half_turn(zero), one))
        for side in range(sides):
            products = jnp.dot(
                whole[side].astype(jnp.bfloat16),
                turned[d, side],
                preferred_element_type=jnp.float32,
            )
            for pair, start in enumerate(starts):
                slot = place[0] * half + sides * pair + side
                block = node_block[d * 2 * half + slot]
                block = jnp.where(slot < live, block, nblocks)
                sums[pair][block] += products[
                    start : start + span, pair * width : (pair + 1) * width
                ]
    atmosphere_core = place[0] == 0
    for k in range(flux_rows):
        nodes = sums[0][:nblocks, k, :]
        for pair in range(1, pairs):
            nodes += sums[pair][:nblocks, k + pair * flux_rows - starts[pair], :]
        cells = flux[k]
        keep[k] = jnp.where(atmosphere_core, nodes, cells)
        give[k] = jnp.where(atmosphere_core, cells, nodes)


def on_device(surface_fields, cell_area, remap_tiles, pair_blocks, slot_cell, node_block):
    rank_count = lax.axis_size("rank")
    digit = math.isqrt(rank_count)
    fields = surface_fields[0]
    width = remap_tiles.shape[1]
    pair_slots = slot_cell.shape[2]
    half = pair_slots // 2
    pairs = half // 2
    field_rows, points = fields.shape
    flux_rows = field_rows // 2
    nblocks = points // width
    by_block = (nblocks, width)
    core = lax.axis_index("comp")
    place = jnp.stack([core, lax.axis_index("rank")]).astype(jnp.int32)
    counts = pair_blocks[0]
    slot_nodes = node_block[0]

    def in_vmem(value):
        return pltpu.with_memory_space_constraint(value, pltpu.VMEM)

    def in_hbm(value):
        return pltpu.with_memory_space_constraint(value, pltpu.HBM)

    def call(kernel, name, in_specs, out_shape, scratch_shapes=(), **options):
        return pl.pallas_call(
            kernel,
            in_specs=in_specs,
            out_specs=jax.tree.map(lambda _: VMEM, out_shape),
            out_shape=out_shape,
            scratch_shapes=scratch_shapes,
            compiler_params=PARAMS,
            name=name,
            **options,
        )

    def to_peer(value, phase, step):
        jumps = (step, step * digit) if phase == 0 else (step * digit, step)
        pairs = [
            (part * rank_count + rank, part * rank_count + (rank ^ jump))
            for part, jump in enumerate(jumps)
            for rank in range(rank_count)
        ]
        return in_vmem(lax.ppermute(value, DEVICES, pairs))

    other_fields = swap_cores(fields)
    other_area = swap_cores(cell_area)

    other_fields, other_area = lax.optimization_barrier((other_fields, other_area))

    tiles = call(
        load_kernel,
        "load_tiles",
        [ANY],
        pltpu.VMEM(remap_tiles.shape, jnp.bfloat16),
        [pltpu.SemaphoreType.DMA],
    )(in_hbm(remap_tiles))

    blocks = pltpu.VMEM((digit, pair_slots // 2 * field_rows, width), jnp.bfloat16)
    messages = call(
        forward_kernel,
        "forward_products",
        [SMEM, SMEM, SMEM, VMEM, VMEM, VMEM],
        [blocks] * digit,
        [pltpu.VMEM(fields.shape, jnp.bfloat16)],
    )(place, counts, slot_nodes, fields, other_fields, tiles)

    brought = [to_peer(messages[i], 0, step_of(i, digit)) for i in range(1, digit)]
    held = [messages[0]] + brought
    onward = call(repack_kernel, "repack", [VMEM] * digit, [blocks] * (digit - 1))(*held)
    arrived = [to_peer(onward[i - 1], 1, step_of(i, digit)) for i in range(1, digit)]

    sums = pltpu.VMEM((nblocks, field_rows, width), jnp.float32)
    cells = slot_cell[0].T
    even_sums, odd_sums, surface = call(
        early_kernel, "early_sums", [SMEM, SMEM] + [VMEM] * (2 + digit), [sums] * 3
    )(place, cells, fields, other_fields, *held)

    late, surface = lax.optimization_barrier((place, surface))
    by_core = (rank_count, 2, half, width, width)
    turned = call(
        turn_kernel,
        "turn_tiles",
        [SMEM, ANY],
        pltpu.VMEM((rank_count, 2, width, pairs * width), jnp.bfloat16),
        [
            pltpu.VMEM((rank_count, half, width, width), jnp.bfloat16),
            pltpu.SemaphoreType.DMA,
        ],
    )(late, in_hbm(remap_tiles.reshape(by_core)))
    turned, surface = lax.optimization_barrier((turned, surface))

    by_flux = pltpu.VMEM((flux_rows, nblocks, width), jnp.float32)
    rows = pltpu.VMEM((nblocks, flux_rows, width), jnp.float32)
    sending, ocean_flux, _, _ = call(
        ocean_kernel,
        "ocean_fluxes",
        [SMEM, SMEM] + [VMEM] * (4 + digit),
        [
            pltpu.VMEM((2 * rank_count, pairs * flux_rows, width), jnp.bfloat16),
            by_flux,
            sums,
            sums,
        ],
        [rows, rows, pltpu.VMEM(by_block, jnp.float32)],
        input_output_aliases={4 + digit: 2, 5 + digit: 3},
    )(
        place,
        cells,
        surface,
        cell_area.reshape(by_block),
        other_area.reshape(by_block),
        *arrived,
        even_sums,
        odd_sums,
    )
    returned = in_vmem(
        lax.all_to_all(sending, DEVICES, split_axis=0, concat_axis=0, tiled=True)
    )

    span = -(-flux_rows // 8) * 8
    keep, give = call(
        back_kernel,
        "node_sums",
        [SMEM, SMEM, SMEM, VMEM, VMEM, VMEM],
        [by_flux, by_flux],
        [pltpu.VMEM((nblocks + 1, span, width), jnp.float32)] * pairs,
    )(place, counts, slot_nodes, returned, turned, ocean_flux)

    divisor = jnp.where(core == 1, 1.0, cell_area.reshape(by_block))
    return ((keep + swap_cores(give)) / divisor).reshape(1, flux_rows, points)


def solution(mesh):
    return jax.shard_map(
        on_device,
        mesh=mesh,
        in_specs=(
            P("comp", None, "rank"),
            P("comp", "rank"),
            P("rank", None, None),
            P("rank", None),
            P("rank", None, None),
            P("rank", None),
        ),
        out_specs=P("comp", None, "rank"),
        check_vma=False,
    )
```

```python
import math

import jax
import jax.numpy as jnp
from jax import lax
from jax.experimental import pallas as pl
from jax.experimental.pallas import tpu as pltpu
from jax.sharding import PartitionSpec as P

FLUX_IT = 5
DEVICES = ("comp", "rank")
SMEM = pl.BlockSpec(memory_space=pltpu.SMEM)
VMEM = pl.BlockSpec(memory_space=pltpu.VMEM)
ANY = pl.BlockSpec(memory_space=pl.ANY)
PARAMS = pltpu.CompilerParams(vmem_limit_bytes=24 << 20)


def swap_cores(value):
    return lax.ppermute(value, "comp", [(0, 1), (1, 0)])


def low_lanes(shape):
    return lax.broadcasted_iota(jnp.int32, shape, len(shape) - 1) < shape[-1] // 2


def half_turn(value):
    return pltpu.roll(value, value.shape[-1] // 2, value.ndim - 1)


def load_kernel(tiles, counts, node_block, slot_cell, *refs):
    *held, place, sems = refs
    copies = [
        pltpu.make_async_copy(source, target, sems.at[i])
        for i, (source, target) in enumerate(
            zip((tiles, counts, node_block, slot_cell), held, strict=True)
        )
    ]
    for copy in copies:
        copy.start()
    place[0] = lax.axis_index("comp")
    place[1] = lax.axis_index("rank")
    for copy in copies:
        copy.wait()


def step_of(index, digit):
    return -index % digit


def peer_of(place, first, second, digit):
    return place[1] ^ jnp.where(place[0] == 0, first + digit * second, digit * first + second)


def forward_kernel(place, counts, node_block, mine, other, tiles, *refs):
    *messages, fields = refs
    digit = len(messages)
    field_rows, width = fields.shape[0], tiles.shape[2]
    pair_slots = tiles.shape[0] // digit**2
    low = low_lanes((field_rows, width))
    own = low == (place[0] == 0)

    @pl.when(place[0] == 0)
    def _():
        fields[...] = mine[...]

    @pl.when(place[0] == 1)
    def _():
        fields[...] = other[...]

    for index in reversed(range(digit)):
        for second in range(digit):
            peer = peer_of(place, step_of(index, digit), second, digit)
            live = counts[peer]
            rows = []
            for slot in range(0, pair_slots, 2):
                at = peer * pair_slots + slot
                sources = [
                    fields[:, pl.ds(pl.multiple_of(node_block[at + i] * width, width), width)]
                    for i in range(2)
                ]
                products = jnp.dot(
                    jnp.concatenate(sources, axis=0),
                    jnp.concatenate([tiles[at], tiles[at + 1]], axis=1),
                    preferred_element_type=jnp.float32,
                )
                even = jnp.where(slot < live, products[:field_rows, :width], 0.0)
                odd = jnp.where(slot + 1 < live, products[field_rows:, width:], 0.0)
                turned = half_turn(jnp.where(low, odd, even))
                rows.append(jnp.where(own, jnp.where(low, even, odd), turned))
            messages[index][second] = jnp.concatenate(rows, axis=0).astype(messages[0].dtype)


def repack_kernel(*refs):
    digit = (len(refs) + 1) // 2
    held, out = refs[:digit], refs[digit:]
    for index in range(1, digit):
        for first in range(digit):
            out[index - 1][first] = held[first][step_of(index, digit)]


def turn_kernel(place, tiles, out, held, sem):
    copy = pltpu.make_async_copy(tiles.at[:, place[0]], held, sem)
    copy.start()
    copy.wait()
    rank_count, sides, width, wide = out.shape
    pairs = wide // width
    for d in range(rank_count):
        for side in range(sides):
            for pair in range(pairs):
                turned = held[d, sides * pair + side].T
                out[d, side, :, pair * width : (pair + 1) * width] = turned


def add_entries(message, slot_cell, source, even_sums, odd_sums):
    field_rows = even_sums.shape[1]
    rows = message.astype(jnp.float32)
    for slot in range(0, slot_cell.shape[0], 2):
        entry = rows[slot // 2 * field_rows : (slot // 2 + 1) * field_rows]
        even_sums[slot_cell[slot, source]] += entry
        odd_sums[slot_cell[slot + 1, source]] += entry


def early_kernel(place, slot_cell, mine, other, *refs):
    *held, even_sums, odd_sums, surface = refs
    digit = len(held)
    nblocks, field_rows, width = surface.shape
    ocean_core = place[0] == 1
    own = low_lanes((field_rows, width)) != ocean_core
    even_sums[...] = jnp.zeros_like(even_sums)
    odd_sums[...] = jnp.zeros_like(odd_sums)
    for index in range(digit):
        source = peer_of(place, step_of(index, digit), 0, digit)
        add_entries(held[index][0], slot_cell, source, even_sums, odd_sums)
    for block in range(nblocks):
        columns = slice(block * width, (block + 1) * width)
        values = jnp.where(ocean_core, mine[:, columns], other[:, columns]).astype(jnp.float32)
        surface[block] = jnp.where(own, values, half_turn(values))


def ocean_kernel(place, slot_cell, surface, own_area, other_area, *refs):
    *arrived, _, _, sending, flux, even_sums, odd_sums, near, far, pull = refs
    digit = len(arrived) + 1
    nblocks, field_rows, width = surface.shape
    flux_rows = field_rows // 2
    pair_slots, rank_count = slot_cell.shape
    half = pair_slots // 2
    ocean_core = place[0] == 1

    for index in range(1, digit):
        for first in range(digit):
            source = peer_of(place, step_of(first, digit), step_of(index, digit), digit)
            add_entries(arrived[index - 1][first], slot_cell, source, even_sums, odd_sums)

    low = low_lanes((field_rows, width))
    for block in range(nblocks):
        mixed = jnp.where(low, even_sums[block], odd_sums[block])
        remapped = mixed + half_turn(mixed)
        near[block] = remapped[:flux_rows] - surface[block, :flux_rows]
        far[block] = (remapped * surface[block])[flux_rows:]

    wind_u, wind_v, excess = near[:, 0, :], near[:, 1, :], near[:, 2, :]
    wind_speed = jnp.sqrt(wind_u * wind_u + wind_v * wind_v + 0.25)
    stability = 1.0 + 4.0 * jax.nn.sigmoid(excess)
    transfer = jnp.ones_like(wind_speed)
    for sweep in range(FLUX_IT):
        transfer = 1.0 / (1.0 + stability * transfer)
    pull[...] = transfer * wind_speed

    own = low_lanes((flux_rows, width)) != ocean_core
    own_rows = low_lanes((nblocks, width)) != ocean_core
    area = jnp.where(ocean_core, own_area[...], other_area[...])
    area = jnp.where(own_rows, area, half_turn(area))
    for block in range(nblocks):
        value = pull[block : block + 1] * near[block] + far[block]
        flux[:, block, :] = jnp.where(own, value, 0.0)
        far[block] = value * area[block : block + 1]

    low = low[:flux_rows]
    for source in range(rank_count):
        for part in range(2):
            rows = []
            for pair in range(half // 2):
                slot = part * half + 2 * pair
                even, odd = slot_cell[slot, source], slot_cell[slot + 1, source]
                rows.append(jnp.where(low, far[even], far[odd]))
            sending[part * rank_count + source] = jnp.concatenate(rows, axis=0).astype(
                sending.dtype
            )


def back_kernel(place, counts, node_block, pieces, turned, flux, keep, give, *sums):
    rank_count, sides, width, _ = turned.shape
    rows = pieces.shape[1]
    flux_rows, nblocks, _ = flux.shape
    pairs = rows // flux_rows
    half = sides * pairs
    span = sums[0].shape[1]
    starts = [pair * flux_rows // 8 * 8 for pair in range(pairs)]
    low = low_lanes((rows, width))
    for total in sums:
        total[...] = jnp.zeros_like(total)
    for d in range(rank_count):
        live = counts[d]
        zero = pieces[d].astype(jnp.float32)
        one = pieces[rank_count + d].astype(jnp.float32)
        whole = (jnp.where(low, zero, half_turn(one)), jnp.where(low, half_turn(zero), one))
        for side in range(sides):
            products = jnp.dot(
                whole[side].astype(jnp.bfloat16),
                turned[d, side],
                preferred_element_type=jnp.float32,
            )
            for pair, start in enumerate(starts):
                slot = place[0] * half + sides * pair + side
                block = node_block[d * 2 * half + slot]
                block = jnp.where(slot < live, block, nblocks)
                sums[pair][block] += products[
                    start : start + span, pair * width : (pair + 1) * width
                ]
    atmosphere_core = place[0] == 0
    for k in range(flux_rows):
        nodes = sums[0][:nblocks, k, :]
        for pair in range(1, pairs):
            nodes += sums[pair][:nblocks, k + pair * flux_rows - starts[pair], :]
        cells = flux[k]
        keep[k] = jnp.where(atmosphere_core, nodes, cells)
        give[k] = jnp.where(atmosphere_core, cells, nodes)


def on_device(surface_fields, cell_area, remap_tiles, pair_blocks, slot_cell, node_block):
    rank_count = lax.axis_size("rank")
    digit = math.isqrt(rank_count)
    fields = surface_fields[0]
    width = remap_tiles.shape[1]
    pair_slots = slot_cell.shape[2]
    half = pair_slots // 2
    pairs = half // 2
    field_rows, points = fields.shape
    flux_rows = field_rows // 2
    nblocks = points // width
    by_block = (nblocks, width)
    core = lax.axis_index("comp")

    def in_vmem(value):
        return pltpu.with_memory_space_constraint(value, pltpu.VMEM)

    def in_hbm(value):
        return pltpu.with_memory_space_constraint(value, pltpu.HBM)

    def call(kernel, name, in_specs, out_shape, scratch_shapes=(), **options):
        return pl.pallas_call(
            kernel,
            in_specs=in_specs,
            out_specs=jax.tree.map(lambda out: pl.BlockSpec(memory_space=out.memory_space), out_shape),
            out_shape=out_shape,
            scratch_shapes=scratch_shapes,
            compiler_params=PARAMS,
            name=name,
            **options,
        )

    def to_peer(value, phase, step):
        jumps = (step, step * digit) if phase == 0 else (step * digit, step)
        pairs = [
            (part * rank_count + rank, part * rank_count + (rank ^ jump))
            for part, jump in enumerate(jumps)
            for rank in range(rank_count)
        ]
        return in_vmem(lax.ppermute(value, DEVICES, pairs))

    other_fields = swap_cores(fields)
    other_area = swap_cores(cell_area)

    other_fields, other_area = lax.optimization_barrier((other_fields, other_area))

    operands = [remap_tiles, pair_blocks[0], node_block[0], slot_cell[0].T]
    tiles, *tables = call(
        load_kernel,
        "load_tiles",
        [ANY] * 4,
        [pltpu.VMEM(remap_tiles.shape, jnp.bfloat16)]
        + [pltpu.SMEM(table.shape, jnp.int32) for table in operands[1:]]
        + [pltpu.SMEM((2,), jnp.int32)],
        [pltpu.SemaphoreType.DMA((4,))],
    )(*map(in_hbm, operands))
    counts, slot_nodes, cells, place = [
        pltpu.with_memory_space_constraint(table, pltpu.SMEM) for table in tables
    ]

    blocks = pltpu.VMEM((digit, pair_slots // 2 * field_rows, width), jnp.bfloat16)
    messages = call(
        forward_kernel,
        "forward_products",
        [SMEM, SMEM, SMEM, VMEM, VMEM, VMEM],
        [blocks] * digit,
        [pltpu.VMEM(fields.shape, jnp.bfloat16)],
    )(place, counts, slot_nodes, fields, other_fields, tiles)

    brought = [to_peer(messages[i], 0, step_of(i, digit)) for i in range(1, digit)]
    held = [messages[0]] + brought
    onward = call(repack_kernel, "repack", [VMEM] * digit, [blocks] * (digit - 1))(*held)
    arrived = [to_peer(onward[i - 1], 1, step_of(i, digit)) for i in range(1, digit)]

    sums = pltpu.VMEM((nblocks, field_rows, width), jnp.float32)
    even_sums, odd_sums, surface = call(
        early_kernel, "early_sums", [SMEM, SMEM] + [VMEM] * (2 + digit), [sums] * 3
    )(place, cells, fields, other_fields, *held)

    turned_tiles, surface = lax.optimization_barrier((remap_tiles, surface))
    by_core = (rank_count, 2, half, width, width)
    turned = call(
        turn_kernel,
        "turn_tiles",
        [SMEM, ANY],
        pltpu.VMEM((rank_count, 2, width, pairs * width), jnp.bfloat16),
        [
            pltpu.VMEM((rank_count, half, width, width), jnp.bfloat16),
            pltpu.SemaphoreType.DMA,
        ],
    )(place, in_hbm(turned_tiles.reshape(by_core)))
    turned, surface = lax.optimization_barrier((turned, surface))

    by_flux = pltpu.VMEM((flux_rows, nblocks, width), jnp.float32)
    rows = pltpu.VMEM((nblocks, flux_rows, width), jnp.float32)
    sending, ocean_flux, _, _ = call(
        ocean_kernel,
        "ocean_fluxes",
        [SMEM, SMEM] + [VMEM] * (4 + digit),
        [
            pltpu.VMEM((2 * rank_count, pairs * flux_rows, width), jnp.bfloat16),
            by_flux,
            sums,
            sums,
        ],
        [rows, rows, pltpu.VMEM(by_block, jnp.float32)],
        input_output_aliases={4 + digit: 2, 5 + digit: 3},
    )(
        place,
        cells,
        surface,
        cell_area.reshape(by_block),
        other_area.reshape(by_block),
        *arrived,
        even_sums,
        odd_sums,
    )
    returned = in_vmem(
        lax.all_to_all(sending, DEVICES, split_axis=0, concat_axis=0, tiled=True)
    )

    span = -(-flux_rows // 8) * 8
    keep, give = call(
        back_kernel,
        "node_sums",
        [SMEM, SMEM, SMEM, VMEM, VMEM, VMEM],
        [by_flux, by_flux],
        [pltpu.VMEM((nblocks + 1, span, width), jnp.float32)] * pairs,
    )(place, counts, slot_nodes, returned, turned, ocean_flux)

    divisor = jnp.where(core == 1, 1.0, cell_area.reshape(by_block))
    return ((keep + swap_cores(give)) / divisor).reshape(1, flux_rows, points)


def solution(mesh):
    return jax.shard_map(
        on_device,
        mesh=mesh,
        in_specs=(
            P("comp", None, "rank"),
            P("comp", "rank"),
            P("rank", None, None),
            P("rank", None),
            P("rank", None, None),
            P("rank", None),
        ),
        out_specs=P("comp", None, "rank"),
        check_vma=False,
    )
```

```python
import functools
import math

import jax
import jax.numpy as jnp
from jax import lax
from jax.experimental import pallas as pl
from jax.experimental.pallas import tpu as pltpu
from jax.sharding import PartitionSpec as P

FLUX_IT = 5
DEVICES = ("comp", "rank")
SMEM = pl.BlockSpec(memory_space=pltpu.SMEM)
VMEM = pl.BlockSpec(memory_space=pltpu.VMEM)
ANY = pl.BlockSpec(memory_space=pl.ANY)
PARAMS = pltpu.CompilerParams(vmem_limit_bytes=24 << 20)


def swap_cores(value):
    return lax.ppermute(value, "comp", [(0, 1), (1, 0)])


def low_lanes(shape):
    return lax.broadcasted_iota(jnp.int32, shape, len(shape) - 1) < shape[-1] // 2


def half_turn(value):
    return pltpu.roll(value, value.shape[-1] // 2, value.ndim - 1)


def load_kernel(tiles, counts, node_block, slot_cell, *refs):
    *held, place, sems = refs
    copies = [
        pltpu.make_async_copy(source, target, sems.at[i])
        for i, (source, target) in enumerate(
            zip((tiles, counts, node_block, slot_cell), held, strict=True)
        )
    ]
    for copy in copies:
        copy.start()
    place[0] = lax.axis_index("comp")
    place[1] = lax.axis_index("rank")
    for copy in copies:
        copy.wait()


def step_of(index, digit):
    return -index % digit


def late_step_of(index, digit):
    return digit - 1 if index == 1 else index - 1


def peer_of(place, first, second, digit):
    return place[1] ^ jnp.where(place[0] == 0, first + digit * second, digit * first + second)


def forward_kernel(place, counts, node_block, mine, other, tiles, *refs):
    *messages, fields = refs
    digit = len(messages)
    field_rows, width = fields.shape[0], tiles.shape[2]
    pair_slots = tiles.shape[0] // digit**2
    low = low_lanes((field_rows, width))
    own = low == (place[0] == 0)

    @pl.when(place[0] == 0)
    def _():
        fields[...] = mine[...]

    @pl.when(place[0] == 1)
    def _():
        fields[...] = other[...]

    for index in reversed(range(digit)):
        for second in range(digit):
            peer = peer_of(place, step_of(index, digit), second, digit)
            live = counts[peer]
            rows = []
            for slot in range(0, pair_slots, 2):
                at = peer * pair_slots + slot
                sources = [
                    fields[:, pl.ds(pl.multiple_of(node_block[at + i] * width, width), width)]
                    for i in range(2)
                ]
                products = jnp.dot(
                    jnp.concatenate(sources, axis=0),
                    jnp.concatenate([tiles[at], tiles[at + 1]], axis=1),
                    preferred_element_type=jnp.float32,
                )
                even = jnp.where(slot < live, products[:field_rows, :width], 0.0)
                odd = jnp.where(slot + 1 < live, products[field_rows:, width:], 0.0)
                turned = half_turn(jnp.where(low, odd, even))
                rows.append(jnp.where(own, jnp.where(low, even, odd), turned))
            messages[index][second] = jnp.concatenate(rows, axis=0).astype(messages[0].dtype)


def repack_kernel(*refs):
    digit = (len(refs) + 1) // 2
    held, out = refs[:digit], refs[digit:]
    for index in range(1, digit):
        for first in range(digit):
            out[index - 1][first] = held[first][late_step_of(index, digit)]


def turn_kernel(place, tiles, out, held, sem):
    copy = pltpu.make_async_copy(tiles.at[:, place[0]], held, sem)
    copy.start()
    copy.wait()
    rank_count, sides, width, wide = out.shape
    pairs = wide // width
    for d in range(rank_count):
        for side in range(sides):
            for pair in range(pairs):
                turned = held[d, sides * pair + side].T
                out[d, side, :, pair * width : (pair + 1) * width] = turned


def add_entries(message, slot_cell, source, even_sums, odd_sums):
    field_rows = even_sums.shape[1]
    rows = message.astype(jnp.float32)
    for slot in range(0, slot_cell.shape[0], 2):
        entry = rows[slot // 2 * field_rows : (slot // 2 + 1) * field_rows]
        even_sums[slot_cell[slot, source]] += entry
        odd_sums[slot_cell[slot + 1, source]] += entry


def early_kernel(place, slot_cell, mine, other, *refs):
    *held, even_sums, odd_sums, surface = refs
    digit = len(held)
    nblocks, field_rows, width = surface.shape
    ocean_core = place[0] == 1
    own = low_lanes((field_rows, width)) != ocean_core
    even_sums[...] = jnp.zeros_like(even_sums)
    odd_sums[...] = jnp.zeros_like(odd_sums)
    for index in range(digit):
        source = peer_of(place, step_of(index, digit), 0, digit)
        add_entries(held[index][0], slot_cell, source, even_sums, odd_sums)
    for block in range(nblocks):
        columns = slice(block * width, (block + 1) * width)
        values = jnp.where(ocean_core, mine[:, columns], other[:, columns]).astype(jnp.float32)
        surface[block] = jnp.where(own, values, half_turn(values))


def middle_kernel(index, digit, place, slot_cell, arrived, _, __, even_sums, odd_sums):
    for first in range(digit):
        source = peer_of(place, step_of(first, digit), late_step_of(index, digit), digit)
        add_entries(arrived[first], slot_cell, source, even_sums, odd_sums)


def ocean_kernel(digit, place, slot_cell, surface, own_area, other_area, arrived, *refs):
    _, _, sending, flux, even_sums, odd_sums, near, far, pull = refs
    nblocks, field_rows, width = surface.shape
    flux_rows = field_rows // 2
    pair_slots, rank_count = slot_cell.shape
    half = pair_slots // 2
    ocean_core = place[0] == 1

    middle_kernel(digit - 1, digit, place, slot_cell, arrived, None, None, even_sums, odd_sums)

    low = low_lanes((field_rows, width))
    for block in range(nblocks):
        mixed = jnp.where(low, even_sums[block], odd_sums[block])
        remapped = mixed + half_turn(mixed)
        near[block] = remapped[:flux_rows] - surface[block, :flux_rows]
        far[block] = (remapped * surface[block])[flux_rows:]

    wind_u, wind_v, excess = near[:, 0, :], near[:, 1, :], near[:, 2, :]
    wind_speed = jnp.sqrt(wind_u * wind_u + wind_v * wind_v + 0.25)
    stability = 1.0 + 4.0 * jax.nn.sigmoid(excess)
    transfer = jnp.ones_like(wind_speed)
    for sweep in range(FLUX_IT):
        transfer = 1.0 / (1.0 + stability * transfer)
    pull[...] = transfer * wind_speed

    own = low_lanes((flux_rows, width)) != ocean_core
    own_rows = low_lanes((nblocks, width)) != ocean_core
    area = jnp.where(ocean_core, own_area[...], other_area[...])
    area = jnp.where(own_rows, area, half_turn(area))
    for block in range(nblocks):
        value = pull[block : block + 1] * near[block] + far[block]
        flux[:, block, :] = jnp.where(own, value, 0.0)
        far[block] = value * area[block : block + 1]

    low = low[:flux_rows]
    for source in range(rank_count):
        for part in range(2):
            rows = []
            for pair in range(half // 2):
                slot = part * half + 2 * pair
                even, odd = slot_cell[slot, source], slot_cell[slot + 1, source]
                rows.append(jnp.where(low, far[even], far[odd]))
            sending[part * rank_count + source] = jnp.concatenate(rows, axis=0).astype(
                sending.dtype
            )


def back_kernel(place, counts, node_block, pieces, turned, flux, keep, give, *sums):
    rank_count, sides, width, _ = turned.shape
    rows = pieces.shape[1]
    flux_rows, nblocks, _ = flux.shape
    pairs = rows // flux_rows
    half = sides * pairs
    span = sums[0].shape[1]
    starts = [pair * flux_rows // 8 * 8 for pair in range(pairs)]
    low = low_lanes((rows, width))
    for total in sums:
        total[...] = jnp.zeros_like(total)
    for d in range(rank_count):
        live = counts[d]
        zero = pieces[d].astype(jnp.float32)
        one = pieces[rank_count + d].astype(jnp.float32)
        whole = (jnp.where(low, zero, half_turn(one)), jnp.where(low, half_turn(zero), one))
        for side in range(sides):
            products = jnp.dot(
                whole[side].astype(jnp.bfloat16),
                turned[d, side],
                preferred_element_type=jnp.float32,
            )
            for pair, start in enumerate(starts):
                slot = place[0] * half + sides * pair + side
                block = node_block[d * 2 * half + slot]
                block = jnp.where(slot < live, block, nblocks)
                sums[pair][block] += products[
                    start : start + span, pair * width : (pair + 1) * width
                ]
    atmosphere_core = place[0] == 0
    for k in range(flux_rows):
        nodes = sums[0][:nblocks, k, :]
        for pair in range(1, pairs):
            nodes += sums[pair][:nblocks, k + pair * flux_rows - starts[pair], :]
        cells = flux[k]
        keep[k] = jnp.where(atmosphere_core, nodes, cells)
        give[k] = jnp.where(atmosphere_core, cells, nodes)


def on_device(surface_fields, cell_area, remap_tiles, pair_blocks, slot_cell, node_block):
    rank_count = lax.axis_size("rank")
    digit = math.isqrt(rank_count)
    fields = surface_fields[0]
    width = remap_tiles.shape[1]
    pair_slots = slot_cell.shape[2]
    half = pair_slots // 2
    pairs = half // 2
    field_rows, points = fields.shape
    flux_rows = field_rows // 2
    nblocks = points // width
    by_block = (nblocks, width)
    core = lax.axis_index("comp")

    def in_vmem(value):
        return pltpu.with_memory_space_constraint(value, pltpu.VMEM)

    def in_hbm(value):
        return pltpu.with_memory_space_constraint(value, pltpu.HBM)

    def call(kernel, name, in_specs, out_shape, scratch_shapes=(), **options):
        return pl.pallas_call(
            kernel,
            in_specs=in_specs,
            out_specs=jax.tree.map(lambda out: pl.BlockSpec(memory_space=out.memory_space), out_shape),
            out_shape=out_shape,
            scratch_shapes=scratch_shapes,
            compiler_params=PARAMS,
            name=name,
            **options,
        )

    def to_peer(value, phase, step):
        jumps = (step, step * digit) if phase == 0 else (step * digit, step)
        pairs = [
            (part * rank_count + rank, part * rank_count + (rank ^ jump))
            for part, jump in enumerate(jumps)
            for rank in range(rank_count)
        ]
        return in_vmem(lax.ppermute(value, DEVICES, pairs))

    other_fields = swap_cores(fields)
    other_area = swap_cores(cell_area)

    other_fields, other_area = lax.optimization_barrier((other_fields, other_area))

    operands = [remap_tiles, pair_blocks[0], node_block[0], slot_cell[0].T]
    tiles, *tables = call(
        load_kernel,
        "load_tiles",
        [ANY] * 4,
        [pltpu.VMEM(remap_tiles.shape, jnp.bfloat16)]
        + [pltpu.SMEM(table.shape, jnp.int32) for table in operands[1:]]
        + [pltpu.SMEM((2,), jnp.int32)],
        [pltpu.SemaphoreType.DMA((4,))],
    )(*map(in_hbm, operands))
    counts, slot_nodes, cells, place = [
        pltpu.with_memory_space_constraint(table, pltpu.SMEM) for table in tables
    ]

    blocks = pltpu.VMEM((digit, pair_slots // 2 * field_rows, width), jnp.bfloat16)
    messages = call(
        forward_kernel,
        "forward_products",
        [SMEM, SMEM, SMEM, VMEM, VMEM, VMEM],
        [blocks] * digit,
        [pltpu.VMEM(fields.shape, jnp.bfloat16)],
    )(place, counts, slot_nodes, fields, other_fields, tiles)

    brought = [to_peer(messages[i], 0, step_of(i, digit)) for i in range(1, digit)]
    held = [messages[0]] + brought
    onward = call(repack_kernel, "repack", [VMEM] * digit, [blocks] * (digit - 1))(*held)
    arrived = [to_peer(onward[i - 1], 1, late_step_of(i, digit)) for i in range(1, digit)]

    sums = pltpu.VMEM((nblocks, field_rows, width), jnp.float32)
    even_sums, odd_sums, surface = call(
        early_kernel, "early_sums", [SMEM, SMEM] + [VMEM] * (2 + digit), [sums] * 3
    )(place, cells, fields, other_fields, *held)

    turned_tiles, surface = lax.optimization_barrier((remap_tiles, surface))
    by_core = (rank_count, 2, half, width, width)
    turned = call(
        turn_kernel,
        "turn_tiles",
        [SMEM, ANY],
        pltpu.VMEM((rank_count, 2, width, pairs * width), jnp.bfloat16),
        [
            pltpu.VMEM((rank_count, half, width, width), jnp.bfloat16),
            pltpu.SemaphoreType.DMA,
        ],
    )(place, in_hbm(turned_tiles.reshape(by_core)))
    turned, surface = lax.optimization_barrier((turned, surface))

    by_flux = pltpu.VMEM((flux_rows, nblocks, width), jnp.float32)
    rows = pltpu.VMEM((nblocks, flux_rows, width), jnp.float32)
    for i, value in enumerate(arrived[:-1]):
        even_sums, odd_sums = call(
            functools.partial(middle_kernel, i + 1, digit),
            "middle_sums",
            [SMEM, SMEM, VMEM, VMEM, VMEM],
            [sums, sums],
            input_output_aliases={3: 0, 4: 1},
        )(place, cells, value, even_sums, odd_sums)
    sending, ocean_flux, _, _ = call(
        functools.partial(ocean_kernel, digit),
        "ocean_fluxes",
        [SMEM, SMEM] + [VMEM] * 6,
        [
            pltpu.VMEM((2 * rank_count, pairs * flux_rows, width), jnp.bfloat16),
            by_flux,
            sums,
            sums,
        ],
        [rows, rows, pltpu.VMEM(by_block, jnp.float32)],
        input_output_aliases={6: 2, 7: 3},
    )(
        place,
        cells,
        surface,
        cell_area.reshape(by_block),
        other_area.reshape(by_block),
        arrived[-1],
        even_sums,
        odd_sums,
    )
    returned = in_vmem(
        lax.all_to_all(sending, DEVICES, split_axis=0, concat_axis=0, tiled=True)
    )

    span = -(-flux_rows // 8) * 8
    keep, give = call(
        back_kernel,
        "node_sums",
        [SMEM, SMEM, SMEM, VMEM, VMEM, VMEM],
        [by_flux, by_flux],
        [pltpu.VMEM((nblocks + 1, span, width), jnp.float32)] * pairs,
    )(place, counts, slot_nodes, returned, turned, ocean_flux)

    divisor = jnp.where(core == 1, 1.0, cell_area.reshape(by_block))
    return ((keep + swap_cores(give)) / divisor).reshape(1, flux_rows, points)


def solution(mesh):
    return jax.shard_map(
        on_device,
        mesh=mesh,
        in_specs=(
            P("comp", None, "rank"),
            P("comp", "rank"),
            P("rank", None, None),
            P("rank", None),
            P("rank", None, None),
            P("rank", None),
        ),
        out_specs=P("comp", None, "rank"),
        check_vma=False,
    )
```

```python
import functools
import itertools
import math

import jax
import jax.numpy as jnp
from jax import lax
from jax.experimental import pallas as pl
from jax.experimental.pallas import tpu as pltpu
from jax.sharding import PartitionSpec as P

FLUX_IT = 5
DEVICES = ("comp", "rank")
SMEM = pl.BlockSpec(memory_space=pltpu.SMEM)
VMEM = pl.BlockSpec(memory_space=pltpu.VMEM)
ANY = pl.BlockSpec(memory_space=pl.ANY)
PARAMS = pltpu.CompilerParams(vmem_limit_bytes=24 << 20)


def swap_cores(value):
    return lax.ppermute(value, "comp", [(0, 1), (1, 0)])


def low_lanes(shape):
    return lax.broadcasted_iota(jnp.int32, shape, len(shape) - 1) < shape[-1] // 2


def half_turn(value):
    return pltpu.roll(value, value.shape[-1] // 2, value.ndim - 1)


def step_of(index, digit):
    return -index % digit


def late_step_of(index, digit):
    return digit - 1 if index == 1 else index - 1


def peer_of(place, first, second, digit):
    return place[1] ^ jnp.where(place[0] == 0, first + digit * second, digit * first + second)


def tile_copies(digit, here, steps, tiles, held, sems):
    count = tiles.shape[0] // digit**2
    copies = []
    for at, (first, second) in enumerate(itertools.product(steps, range(digit))):
        peer = peer_of(here, first, second, digit)
        source = tiles.at[pl.ds(peer * count, count)]
        copies.append(
            pltpu.make_async_copy(source, held.at[at * count : (at + 1) * count], sems.at[at])
        )
    return copies


def load_kernel(digit, steps, tiles, counts, node_block, slot_cell, *refs):
    *held, place, kept, sems, tile_sems = refs
    here = lax.axis_index("comp"), lax.axis_index("rank")
    copies = [
        pltpu.make_async_copy(source, target, sems.at[i])
        for i, (source, target) in enumerate(
            zip((counts, node_block, slot_cell), held, strict=True)
        )
    ]
    copies += tile_copies(digit, here, steps, tiles, kept, tile_sems)
    for copy in copies:
        copy.start()
    place[0], place[1] = here
    for copy in copies:
        copy.wait()


def choose_kernel(place, mine, other, fields):
    @pl.when(place[0] == 0)
    def _():
        fields[...] = mine[...]

    @pl.when(place[0] == 1)
    def _():
        fields[...] = other[...]


def forward_kernel(digit, steps, place, counts, node_block, fields, tiles, *messages):
    field_rows, width = fields.shape[0], tiles.shape[2]
    pair_slots = node_block.shape[0] // digit**2
    low = low_lanes((field_rows, width))
    own = low == (place[0] == 0)
    for index, (message, first) in enumerate(zip(messages, steps, strict=True)):
        for second in range(digit):
            peer = peer_of(place, first, second, digit)
            tile = (index * digit + second) * pair_slots
            live = counts[peer]
            rows = []
            for slot in range(0, pair_slots, 2):
                at = peer * pair_slots + slot
                sources = []
                for i in range(2):
                    columns = pl.ds(pl.multiple_of(node_block[at + i] * width, width), width)
                    sources.append(fields[:, columns])
                products = jnp.dot(
                    jnp.concatenate(sources, axis=0),
                    jnp.concatenate([tiles[tile + slot], tiles[tile + slot + 1]], axis=1),
                    preferred_element_type=jnp.float32,
                )
                even = jnp.where(slot < live, products[:field_rows, :width], 0.0)
                odd = jnp.where(slot + 1 < live, products[field_rows:, width:], 0.0)
                turned = half_turn(jnp.where(low, odd, even))
                rows.append(jnp.where(own, jnp.where(low, even, odd), turned))
            message[second] = jnp.concatenate(rows, axis=0).astype(message.dtype)


def own_kernel(digit, place, counts, node_block, fields, tiles, message, held, sems):
    copies = tile_copies(digit, (place[0], place[1]), [0], tiles, held, sems)
    for copy in copies:
        copy.start()
    for copy in copies:
        copy.wait()
    forward_kernel(digit, [0], place, counts, node_block, fields, held, message)


def repack_kernel(*refs):
    digit = (len(refs) + 1) // 2
    held, out = refs[:digit], refs[digit:]
    for index in range(1, digit):
        for first in range(digit):
            out[index - 1][first] = held[first][late_step_of(index, digit)]


def turn_kernel(place, tiles, out, held, sem):
    copy = pltpu.make_async_copy(tiles.at[:, place[0]], held, sem)
    copy.start()
    copy.wait()
    rank_count, sides, width, wide = out.shape
    pairs = wide // width
    for d in range(rank_count):
        for side in range(sides):
            for pair in range(pairs):
                turned = held[d, sides * pair + side].T
                out[d, side, :, pair * width : (pair + 1) * width] = turned


def add_entries(message, slot_cell, source, even_sums, odd_sums):
    field_rows = even_sums.shape[1]
    rows = message.astype(jnp.float32)
    for slot in range(0, slot_cell.shape[0], 2):
        entry = rows[slot // 2 * field_rows : (slot // 2 + 1) * field_rows]
        even_sums[slot_cell[slot, source]] += entry
        odd_sums[slot_cell[slot + 1, source]] += entry


def early_kernel(place, slot_cell, mine, other, *refs):
    *held, even_sums, odd_sums, surface = refs
    digit = len(held)
    nblocks, field_rows, width = surface.shape
    ocean_core = place[0] == 1
    own = low_lanes((field_rows, width)) != ocean_core
    even_sums[...] = jnp.zeros_like(even_sums)
    odd_sums[...] = jnp.zeros_like(odd_sums)
    for index in range(digit):
        source = peer_of(place, step_of(index, digit), 0, digit)
        add_entries(held[index][0], slot_cell, source, even_sums, odd_sums)
    for block in range(nblocks):
        columns = slice(block * width, (block + 1) * width)
        values = jnp.where(ocean_core, mine[:, columns], other[:, columns]).astype(jnp.float32)
        surface[block] = jnp.where(own, values, half_turn(values))


def middle_kernel(index, digit, place, slot_cell, arrived, _, __, even_sums, odd_sums):
    for first in range(digit):
        source = peer_of(place, step_of(first, digit), late_step_of(index, digit), digit)
        add_entries(arrived[first], slot_cell, source, even_sums, odd_sums)


def ocean_kernel(digit, place, slot_cell, surface, own_area, other_area, arrived, *refs):
    _, _, sending, flux, even_sums, odd_sums, near, far, pull = refs
    nblocks, field_rows, width = surface.shape
    flux_rows = field_rows // 2
    pair_slots, rank_count = slot_cell.shape
    half = pair_slots // 2
    ocean_core = place[0] == 1

    middle_kernel(digit - 1, digit, place, slot_cell, arrived, None, None, even_sums, odd_sums)

    low = low_lanes((field_rows, width))
    for block in range(nblocks):
        mixed = jnp.where(low, even_sums[block], odd_sums[block])
        remapped = mixed + half_turn(mixed)
        near[block] = remapped[:flux_rows] - surface[block, :flux_rows]
        far[block] = (remapped * surface[block])[flux_rows:]

    wind_u, wind_v, excess = near[:, 0, :], near[:, 1, :], near[:, 2, :]
    wind_speed = jnp.sqrt(wind_u * wind_u + wind_v * wind_v + 0.25)
    stability = 1.0 + 4.0 * jax.nn.sigmoid(excess)
    transfer = jnp.ones_like(wind_speed)
    for sweep in range(FLUX_IT):
        transfer = 1.0 / (1.0 + stability * transfer)
    pull[...] = transfer * wind_speed

    own = low_lanes((flux_rows, width)) != ocean_core
    own_rows = low_lanes((nblocks, width)) != ocean_core
    area = jnp.where(ocean_core, own_area[...], other_area[...])
    area = jnp.where(own_rows, area, half_turn(area))
    for block in range(nblocks):
        value = pull[block : block + 1] * near[block] + far[block]
        flux[:, block, :] = jnp.where(own, value, 0.0)
        far[block] = value * area[block : block + 1]

    low = low[:flux_rows]
    for source in range(rank_count):
        for part in range(2):
            rows = []
            for pair in range(half // 2):
                slot = part * half + 2 * pair
                even, odd = slot_cell[slot, source], slot_cell[slot + 1, source]
                rows.append(jnp.where(low, far[even], far[odd]))
            sending[part * rank_count + source] = jnp.concatenate(rows, axis=0).astype(
                sending.dtype
            )


def back_kernel(place, counts, node_block, pieces, turned, flux, keep, give, *sums):
    rank_count, sides, width, _ = turned.shape
    rows = pieces.shape[1]
    flux_rows, nblocks, _ = flux.shape
    pairs = rows // flux_rows
    half = sides * pairs
    span = sums[0].shape[1]
    starts = [pair * flux_rows // 8 * 8 for pair in range(pairs)]
    low = low_lanes((rows, width))
    for total in sums:
        total[...] = jnp.zeros_like(total)
    for d in range(rank_count):
        live = counts[d]
        zero = pieces[d].astype(jnp.float32)
        one = pieces[rank_count + d].astype(jnp.float32)
        whole = (jnp.where(low, zero, half_turn(one)), jnp.where(low, half_turn(zero), one))
        for side in range(sides):
            products = jnp.dot(
                whole[side].astype(jnp.bfloat16),
                turned[d, side],
                preferred_element_type=jnp.float32,
            )
            for pair, start in enumerate(starts):
                slot = place[0] * half + sides * pair + side
                block = node_block[d * 2 * half + slot]
                block = jnp.where(slot < live, block, nblocks)
                sums[pair][block] += products[
                    start : start + span, pair * width : (pair + 1) * width
                ]
    atmosphere_core = place[0] == 0
    for k in range(flux_rows):
        nodes = sums[0][:nblocks, k, :]
        for pair in range(1, pairs):
            nodes += sums[pair][:nblocks, k + pair * flux_rows - starts[pair], :]
        cells = flux[k]
        keep[k] = jnp.where(atmosphere_core, nodes, cells)
        give[k] = jnp.where(atmosphere_core, cells, nodes)


def on_device(surface_fields, cell_area, remap_tiles, pair_blocks, slot_cell, node_block):
    rank_count = lax.axis_size("rank")
    digit = math.isqrt(rank_count)
    fields = surface_fields[0]
    width = remap_tiles.shape[1]
    pair_slots = slot_cell.shape[2]
    half = pair_slots // 2
    pairs = half // 2
    field_rows, points = fields.shape
    flux_rows = field_rows // 2
    nblocks = points // width
    by_block = (nblocks, width)
    core = lax.axis_index("comp")

    def in_vmem(value):
        return pltpu.with_memory_space_constraint(value, pltpu.VMEM)

    def in_hbm(value):
        return pltpu.with_memory_space_constraint(value, pltpu.HBM)

    def call(kernel, name, in_specs, out_shape, scratch_shapes=(), **options):
        return pl.pallas_call(
            kernel,
            in_specs=in_specs,
            out_specs=jax.tree.map(lambda out: pl.BlockSpec(memory_space=out.memory_space), out_shape),
            out_shape=out_shape,
            scratch_shapes=scratch_shapes,
            compiler_params=PARAMS,
            name=name,
            **options,
        )

    def to_peer(value, phase, step):
        jumps = (step, step * digit) if phase == 0 else (step * digit, step)
        pairs = [
            (part * rank_count + rank, part * rank_count + (rank ^ jump))
            for part, jump in enumerate(jumps)
            for rank in range(rank_count)
        ]
        return in_vmem(lax.ppermute(value, DEVICES, pairs))

    other_fields = swap_cores(fields)
    other_area = swap_cores(cell_area)

    other_fields, other_area = lax.optimization_barrier((other_fields, other_area))

    def part(steps):
        count = len(steps) * digit
        return [
            pltpu.VMEM((count * pair_slots, width, width), jnp.bfloat16),
            pltpu.SemaphoreType.DMA((count,)),
        ]

    steps = [step_of(i, digit) for i in range(1, digit)]
    operands = [remap_tiles, pair_blocks[0], node_block[0], slot_cell[0].T]
    loaded, load_sems = part(steps)
    *tables, tiles = call(
        functools.partial(load_kernel, digit, steps),
        "load_tiles",
        [ANY] * 4,
        [pltpu.SMEM(table.shape, jnp.int32) for table in operands[1:]]
        + [pltpu.SMEM((2,), jnp.int32), loaded],
        [pltpu.SemaphoreType.DMA((3,)), load_sems],
    )(*map(in_hbm, operands))
    counts, slot_nodes, cells, place = [
        pltpu.with_memory_space_constraint(table, pltpu.SMEM) for table in tables
    ]

    blocks = pltpu.VMEM((digit, pair_slots // 2 * field_rows, width), jnp.bfloat16)
    atmosphere = call(
        choose_kernel, "atmosphere", [SMEM, VMEM, VMEM], pltpu.VMEM(fields.shape, jnp.bfloat16)
    )(place, fields, other_fields)

    messages = call(
        functools.partial(forward_kernel, digit, steps),
        "forward_products",
        [SMEM, SMEM, SMEM, VMEM, VMEM],
        [blocks] * len(steps),
    )(place, counts, slot_nodes, atmosphere, tiles)
    at_home = call(
        functools.partial(own_kernel, digit),
        "own_products",
        [SMEM, SMEM, SMEM, VMEM, ANY],
        blocks,
        part([0]),
    )(place, counts, slot_nodes, atmosphere, in_hbm(remap_tiles))
    brought = [to_peer(value, 0, step) for value, step in zip(messages, steps, strict=True)]
    held = [at_home] + brought
    onward = call(repack_kernel, "repack", [VMEM] * digit, [blocks] * (digit - 1))(*held)
    arrived = [to_peer(onward[i - 1], 1, late_step_of(i, digit)) for i in range(1, digit)]

    sums = pltpu.VMEM((nblocks, field_rows, width), jnp.float32)
    even_sums, odd_sums, surface = call(
        early_kernel, "early_sums", [SMEM, SMEM] + [VMEM] * (2 + digit), [sums] * 3
    )(place, cells, fields, other_fields, *held)

    turned_tiles, surface = lax.optimization_barrier((remap_tiles, surface))
    by_core = (rank_count, 2, half, width, width)
    turned = call(
        turn_kernel,
        "turn_tiles",
        [SMEM, ANY],
        pltpu.VMEM((rank_count, 2, width, pairs * width), jnp.bfloat16),
        [
            pltpu.VMEM((rank_count, half, width, width), jnp.bfloat16),
            pltpu.SemaphoreType.DMA,
        ],
    )(place, in_hbm(turned_tiles.reshape(by_core)))
    turned, surface = lax.optimization_barrier((turned, surface))

    by_flux = pltpu.VMEM((flux_rows, nblocks, width), jnp.float32)
    rows = pltpu.VMEM((nblocks, flux_rows, width), jnp.float32)
    for i, value in enumerate(arrived[:-1]):
        even_sums, odd_sums = call(
            functools.partial(middle_kernel, i + 1, digit),
            "middle_sums",
            [SMEM, SMEM, VMEM, VMEM, VMEM],
            [sums, sums],
            input_output_aliases={3: 0, 4: 1},
        )(place, cells, value, even_sums, odd_sums)
    sending, ocean_flux, _, _ = call(
        functools.partial(ocean_kernel, digit),
        "ocean_fluxes",
        [SMEM, SMEM] + [VMEM] * 6,
        [
            pltpu.VMEM((2 * rank_count, pairs * flux_rows, width), jnp.bfloat16),
            by_flux,
            sums,
            sums,
        ],
        [rows, rows, pltpu.VMEM(by_block, jnp.float32)],
        input_output_aliases={6: 2, 7: 3},
    )(
        place,
        cells,
        surface,
        cell_area.reshape(by_block),
        other_area.reshape(by_block),
        arrived[-1],
        even_sums,
        odd_sums,
    )
    returned = in_vmem(
        lax.all_to_all(sending, DEVICES, split_axis=0, concat_axis=0, tiled=True)
    )

    span = -(-flux_rows // 8) * 8
    keep, give = call(
        back_kernel,
        "node_sums",
        [SMEM, SMEM, SMEM, VMEM, VMEM, VMEM],
        [by_flux, by_flux],
        [pltpu.VMEM((nblocks + 1, span, width), jnp.float32)] * pairs,
    )(place, counts, slot_nodes, returned, turned, ocean_flux)

    divisor = jnp.where(core == 1, 1.0, cell_area.reshape(by_block))
    return ((keep + swap_cores(give)) / divisor).reshape(1, flux_rows, points)


def solution(mesh):
    return jax.shard_map(
        on_device,
        mesh=mesh,
        in_specs=(
            P("comp", None, "rank"),
            P("comp", "rank"),
            P("rank", None, None),
            P("rank", None),
            P("rank", None, None),
            P("rank", None),
        ),
        out_specs=P("comp", None, "rank"),
        check_vma=False,
    )
```

```python
import functools
import itertools
import math

import jax
import jax.numpy as jnp
from jax import lax
from jax.experimental import pallas as pl
from jax.experimental.pallas import tpu as pltpu
from jax.sharding import PartitionSpec as P

FLUX_IT = 5
DEVICES = ("comp", "rank")
SMEM = pl.BlockSpec(memory_space=pltpu.SMEM)
VMEM = pl.BlockSpec(memory_space=pltpu.VMEM)
ANY = pl.BlockSpec(memory_space=pl.ANY)
PARAMS = pltpu.CompilerParams(vmem_limit_bytes=24 << 20)


def swap_cores(value):
    return lax.ppermute(value, "comp", [(0, 1), (1, 0)])


def low_lanes(shape):
    return lax.broadcasted_iota(jnp.int32, shape, len(shape) - 1) < shape[-1] // 2


def half_turn(value):
    return pltpu.roll(value, value.shape[-1] // 2, value.ndim - 1)


def step_of(index, digit):
    return -index % digit


def late_step_of(index, digit):
    return digit - 1 if index == 1 else index - 1


def peer_of(place, first, second, digit):
    return place[1] ^ jnp.where(place[0] == 0, first + digit * second, digit * first + second)


def tile_copies(digit, here, steps, tiles, held, sems):
    count = tiles.shape[0] // digit**2
    copies = []
    for at, (first, second) in enumerate(itertools.product(steps, range(digit))):
        peer = peer_of(here, first, second, digit)
        source = tiles.at[pl.ds(peer * count, count)]
        copies.append(
            pltpu.make_async_copy(source, held.at[at * count : (at + 1) * count], sems.at[at])
        )
    return copies


def load_kernel(digit, steps, tiles, counts, node_block, slot_cell, *refs):
    *held, place, kept, sems, tile_sems = refs
    here = lax.axis_index("comp"), lax.axis_index("rank")
    copies = [
        pltpu.make_async_copy(source, target, sems.at[i])
        for i, (source, target) in enumerate(
            zip((counts, node_block, slot_cell), held, strict=True)
        )
    ]
    copies += tile_copies(digit, here, steps, tiles, kept, tile_sems)
    for copy in copies:
        copy.start()
    place[0], place[1] = here
    for copy in copies:
        copy.wait()


def choose_kernel(place, mine, other, fields):
    @pl.when(place[0] == 0)
    def _():
        fields[...] = mine[...]

    @pl.when(place[0] == 1)
    def _():
        fields[...] = other[...]


def forward_kernel(digit, steps, place, counts, node_block, fields, tiles, *messages):
    field_rows, width = fields.shape[0], tiles.shape[2]
    pair_slots = node_block.shape[0] // digit**2
    low = low_lanes((field_rows, width))
    own = low == (place[0] == 0)
    for index, (message, first) in enumerate(zip(messages, steps, strict=True)):
        for second in range(digit):
            peer = peer_of(place, first, second, digit)
            tile = (index * digit + second) * pair_slots
            live = counts[peer]
            rows = []
            for slot in range(0, pair_slots, 2):
                at = peer * pair_slots + slot
                sources = []
                for i in range(2):
                    columns = pl.ds(pl.multiple_of(node_block[at + i] * width, width), width)
                    sources.append(fields[:, columns])
                products = jnp.dot(
                    jnp.concatenate(sources, axis=0),
                    jnp.concatenate([tiles[tile + slot], tiles[tile + slot + 1]], axis=1),
                    preferred_element_type=jnp.float32,
                )
                even = jnp.where(slot < live, products[:field_rows, :width], 0.0)
                odd = jnp.where(slot + 1 < live, products[field_rows:, width:], 0.0)
                turned = half_turn(jnp.where(low, odd, even))
                rows.append(jnp.where(own, jnp.where(low, even, odd), turned))
            message[second] = jnp.concatenate(rows, axis=0).astype(message.dtype)


def own_kernel(digit, place, counts, node_block, fields, tiles, message, held, sems):
    copies = tile_copies(digit, (place[0], place[1]), [0], tiles, held, sems)
    for copy in copies:
        copy.start()
    for copy in copies:
        copy.wait()
    forward_kernel(digit, [0], place, counts, node_block, fields, held, message)


def repack_kernel(*refs):
    digit = (len(refs) + 1) // 2
    held, out = refs[:digit], refs[digit:]
    for index in range(1, digit):
        for first in range(digit):
            out[index - 1][first] = held[first][late_step_of(index, digit)]


def turn_kernel(place, tiles, out, held, sem):
    copy = pltpu.make_async_copy(tiles, held, sem)
    copy.start()
    rank_count, pairs, width, _ = out.shape
    mid = width // 2
    copy.wait()
    for d in range(rank_count):
        for pair in range(pairs):
            for i in range(2):
                turned = held[(d * pairs + pair) * 2 + i].T
                out[d, pair, i * mid : (i + 1) * mid] = jnp.where(
                    place[0] == 0, turned[:mid], turned[mid:]
                )


def add_entries(message, slot_cell, source, even_sums, odd_sums):
    field_rows = even_sums.shape[1]
    rows = message.astype(jnp.float32)
    for slot in range(0, slot_cell.shape[0], 2):
        entry = rows[slot // 2 * field_rows : (slot // 2 + 1) * field_rows]
        even_sums[slot_cell[slot, source]] += entry
        odd_sums[slot_cell[slot + 1, source]] += entry


def early_kernel(place, slot_cell, mine, other, *refs):
    *held, even_sums, odd_sums, surface = refs
    digit = len(held)
    nblocks, field_rows, width = surface.shape
    ocean_core = place[0] == 1
    own = low_lanes((field_rows, width)) != ocean_core
    even_sums[...] = jnp.zeros_like(even_sums)
    odd_sums[...] = jnp.zeros_like(odd_sums)
    for index in range(digit):
        source = peer_of(place, step_of(index, digit), 0, digit)
        add_entries(held[index][0], slot_cell, source, even_sums, odd_sums)
    for block in range(nblocks):
        columns = slice(block * width, (block + 1) * width)
        values = jnp.where(ocean_core, mine[:, columns], other[:, columns]).astype(jnp.float32)
        surface[block] = jnp.where(own, values, half_turn(values))


def middle_kernel(index, digit, place, slot_cell, arrived, _, __, even_sums, odd_sums):
    for first in range(digit):
        source = peer_of(place, step_of(first, digit), late_step_of(index, digit), digit)
        add_entries(arrived[first], slot_cell, source, even_sums, odd_sums)


def ocean_kernel(digit, place, slot_cell, surface, own_area, other_area, arrived, *refs):
    _, _, sending, flux, even_sums, odd_sums, near, far, pull = refs
    nblocks, field_rows, width = surface.shape
    flux_rows = field_rows // 2
    pair_slots, rank_count = slot_cell.shape
    ocean_core = place[0] == 1

    middle_kernel(digit - 1, digit, place, slot_cell, arrived, None, None, even_sums, odd_sums)

    low = low_lanes((field_rows, width))
    for block in range(nblocks):
        mixed = jnp.where(low, even_sums[block], odd_sums[block])
        remapped = mixed + half_turn(mixed)
        near[block] = remapped[:flux_rows] - surface[block, :flux_rows]
        far[block] = (remapped * surface[block])[flux_rows:]

    wind_u, wind_v, excess = near[:, 0, :], near[:, 1, :], near[:, 2, :]
    wind_speed = jnp.sqrt(wind_u * wind_u + wind_v * wind_v + 0.25)
    stability = 1.0 + 4.0 * jax.nn.sigmoid(excess)
    transfer = jnp.ones_like(wind_speed)
    for sweep in range(FLUX_IT):
        transfer = 1.0 / (1.0 + stability * transfer)
    pull[...] = transfer * wind_speed

    own = low_lanes((flux_rows, width)) != ocean_core
    own_rows = low_lanes((nblocks, width)) != ocean_core
    area = jnp.where(ocean_core, own_area[...], other_area[...])
    area = jnp.where(own_rows, area, half_turn(area))
    for block in range(nblocks):
        value = pull[block : block + 1] * near[block] + far[block]
        flux[:, block, :] = jnp.where(own, value, 0.0)
        far[block] = value * area[block : block + 1]

    low = low[:flux_rows]
    for source in range(rank_count):
        rows = []
        for slot in range(0, pair_slots, 2):
            even, odd = slot_cell[slot, source], slot_cell[slot + 1, source]
            rows.append(jnp.where(low, far[even], far[odd]))
        sending[source] = jnp.concatenate(rows, axis=0).astype(sending.dtype)


def back_kernel(core, place, counts, node_block, pieces, turned, flux, out, *sums):
    rank_count, pairs, width, _ = turned.shape
    flux_rows, nblocks, _ = flux.shape
    span = sums[0].shape[1]
    low = low_lanes((span, width))

    @pl.when(place[0] != core)
    def _():
        out[...] = flux[...]

    @pl.when(place[0] == core)
    def _():
        for total in sums:
            total[...] = jnp.zeros_like(total)
        for d in range(rank_count):
            live = counts[d]
            rows = pieces[d].astype(jnp.float32)
            for pair in range(pairs):
                start = pair * flux_rows // 8 * 8
                piece = rows[start : start + span]
                halves = [jnp.where(low, piece, 0.0), jnp.where(low, 0.0, piece)]
                products = jnp.dot(
                    jnp.concatenate(halves, axis=0).astype(jnp.bfloat16),
                    turned[d, pair],
                    preferred_element_type=jnp.float32,
                )
                total = sums[(pair * flux_rows - start) // 4]
                for i in range(2):
                    slot = 2 * pair + i
                    block = node_block[d * 2 * pairs + slot]
                    block = jnp.where(slot < live, block, nblocks)
                    total[block] += products[i * span : (i + 1) * span]
        for k in range(flux_rows):
            nodes = sums[0][:nblocks, k, :]
            for i, total in enumerate(sums[1:], 1):
                nodes += total[:nblocks, k + 4 * i, :]
            out[k] = nodes


def on_device(surface_fields, cell_area, remap_tiles, pair_blocks, slot_cell, node_block):
    rank_count = lax.axis_size("rank")
    digit = math.isqrt(rank_count)
    fields = surface_fields[0]
    width = remap_tiles.shape[1]
    pair_slots = slot_cell.shape[2]
    pairs = pair_slots // 2
    field_rows, points = fields.shape
    flux_rows = field_rows // 2
    nblocks = points // width
    by_block = (nblocks, width)
    core = lax.axis_index("comp")

    def in_vmem(value):
        return pltpu.with_memory_space_constraint(value, pltpu.VMEM)

    def in_hbm(value):
        return pltpu.with_memory_space_constraint(value, pltpu.HBM)

    def call(kernel, name, in_specs, out_shape, scratch_shapes=(), **options):
        return pl.pallas_call(
            kernel,
            in_specs=in_specs,
            out_specs=jax.tree.map(lambda out: pl.BlockSpec(memory_space=out.memory_space), out_shape),
            out_shape=out_shape,
            scratch_shapes=scratch_shapes,
            compiler_params=PARAMS,
            name=name,
            **options,
        )

    def to_peer(value, phase, step):
        jumps = (step, step * digit) if phase == 0 else (step * digit, step)
        pairs = [
            (part * rank_count + rank, part * rank_count + (rank ^ jump))
            for part, jump in enumerate(jumps)
            for rank in range(rank_count)
        ]
        return in_vmem(lax.ppermute(value, DEVICES, pairs))

    other_fields = swap_cores(fields)
    other_area = swap_cores(cell_area)

    other_fields, other_area = lax.optimization_barrier((other_fields, other_area))

    def part(steps):
        count = len(steps) * digit
        return [
            pltpu.VMEM((count * pair_slots, width, width), jnp.bfloat16),
            pltpu.SemaphoreType.DMA((count,)),
        ]

    steps = [step_of(i, digit) for i in range(1, digit)]
    operands = [remap_tiles, pair_blocks[0], node_block[0], slot_cell[0].T]
    loaded, load_sems = part(steps)
    *tables, tiles = call(
        functools.partial(load_kernel, digit, steps),
        "load_tiles",
        [ANY] * 4,
        [pltpu.SMEM(table.shape, jnp.int32) for table in operands[1:]]
        + [pltpu.SMEM((2,), jnp.int32), loaded],
        [pltpu.SemaphoreType.DMA((3,)), load_sems],
    )(*map(in_hbm, operands))
    counts, slot_nodes, cells, place = [
        pltpu.with_memory_space_constraint(table, pltpu.SMEM) for table in tables
    ]

    blocks = pltpu.VMEM((digit, pair_slots // 2 * field_rows, width), jnp.bfloat16)
    atmosphere = call(
        choose_kernel, "atmosphere", [SMEM, VMEM, VMEM], pltpu.VMEM(fields.shape, jnp.bfloat16)
    )(place, fields, other_fields)

    messages = call(
        functools.partial(forward_kernel, digit, steps),
        "forward_products",
        [SMEM, SMEM, SMEM, VMEM, VMEM],
        [blocks] * len(steps),
    )(place, counts, slot_nodes, atmosphere, tiles)
    at_home = call(
        functools.partial(own_kernel, digit),
        "own_products",
        [SMEM, SMEM, SMEM, VMEM, ANY],
        blocks,
        part([0]),
    )(place, counts, slot_nodes, atmosphere, in_hbm(remap_tiles))
    brought = [to_peer(value, 0, step) for value, step in zip(messages, steps, strict=True)]
    held = [at_home] + brought
    onward = call(repack_kernel, "repack", [VMEM] * digit, [blocks] * (digit - 1))(*held)
    arrived = [to_peer(onward[i - 1], 1, late_step_of(i, digit)) for i in range(1, digit)]

    sums = pltpu.VMEM((nblocks, field_rows, width), jnp.float32)
    even_sums, odd_sums, surface = call(
        early_kernel, "early_sums", [SMEM, SMEM] + [VMEM] * (2 + digit), [sums] * 3
    )(place, cells, fields, other_fields, *held)

    turned_tiles, surface = lax.optimization_barrier((remap_tiles, surface))
    turned = call(
        turn_kernel,
        "turn_tiles",
        [SMEM, ANY],
        pltpu.VMEM((rank_count, pairs, width, width), jnp.bfloat16),
        [pltpu.VMEM(remap_tiles.shape, jnp.bfloat16), pltpu.SemaphoreType.DMA],
    )(place, in_hbm(turned_tiles))
    turned, surface = lax.optimization_barrier((turned, surface))

    by_flux = pltpu.VMEM((flux_rows, nblocks, width), jnp.float32)
    rows = pltpu.VMEM((nblocks, flux_rows, width), jnp.float32)
    for i, value in enumerate(arrived[:-1]):
        even_sums, odd_sums = call(
            functools.partial(middle_kernel, i + 1, digit),
            "middle_sums",
            [SMEM, SMEM, VMEM, VMEM, VMEM],
            [sums, sums],
            input_output_aliases={3: 0, 4: 1},
        )(place, cells, value, even_sums, odd_sums)
    sending, ocean_flux, _, _ = call(
        functools.partial(ocean_kernel, digit),
        "ocean_fluxes",
        [SMEM, SMEM] + [VMEM] * 6,
        [
            pltpu.VMEM((rank_count, pairs * flux_rows, width), jnp.bfloat16),
            by_flux,
            sums,
            sums,
        ],
        [rows, rows, pltpu.VMEM(by_block, jnp.float32)],
        input_output_aliases={6: 2, 7: 3},
    )(
        place,
        cells,
        surface,
        cell_area.reshape(by_block),
        other_area.reshape(by_block),
        arrived[-1],
        even_sums,
        odd_sums,
    )
    returned = lax.all_to_all(sending, "rank", split_axis=0, concat_axis=0, tiled=True)

    span = -(-flux_rows // 8) * 8

    def back(core, name, returned):
        return call(
            functools.partial(back_kernel, core),
            name,
            [SMEM, SMEM, SMEM, VMEM, VMEM, VMEM],
            by_flux,
            [pltpu.VMEM((nblocks + 1, span, width), jnp.float32)] * 2,
        )(place, counts, slot_nodes, in_vmem(returned), turned, ocean_flux)

    give = back(1, "given_sums", returned)
    returned, give = lax.optimization_barrier((returned, give))
    keep = back(0, "kept_sums", returned)
    divisor = jnp.where(core == 1, 1.0, cell_area.reshape(by_block))
    return ((keep + swap_cores(give)) / divisor).reshape(1, flux_rows, points)


def solution(mesh):
    return jax.shard_map(
        on_device,
        mesh=mesh,
        in_specs=(
            P("comp", None, "rank"),
            P("comp", "rank"),
            P("rank", None, None),
            P("rank", None),
            P("rank", None, None),
            P("rank", None),
        ),
        out_specs=P("comp", None, "rank"),
        check_vma=False,
    )
```

```python
import functools
import itertools
import math

import jax
import jax.numpy as jnp
from jax import lax
from jax.experimental import pallas as pl
from jax.experimental.pallas import tpu as pltpu
from jax.sharding import PartitionSpec as P

FLUX_IT = 5
DEVICES = ("comp", "rank")
SMEM = pl.BlockSpec(memory_space=pltpu.SMEM)
VMEM = pl.BlockSpec(memory_space=pltpu.VMEM)
ANY = pl.BlockSpec(memory_space=pl.ANY)
PARAMS = pltpu.CompilerParams(vmem_limit_bytes=24 << 20)


def swap_cores(value):
    return lax.ppermute(value, "comp", [(0, 1), (1, 0)])


def low_lanes(shape):
    return lax.broadcasted_iota(jnp.int32, shape, len(shape) - 1) < shape[-1] // 2


def half_turn(value):
    return pltpu.roll(value, value.shape[-1] // 2, value.ndim - 1)


def step_of(index, digit):
    return digit - 1 if index == 1 else max(index - 1, 0)


def peer_of(place, first, second, digit):
    return place[1] ^ jnp.where(place[0] == 0, first + digit * second, digit * first + second)


def tile_copies(digit, here, steps, tiles, held, sems):
    count = tiles.shape[0] // digit**2
    copies = []
    for at, (first, second) in enumerate(itertools.product(steps, range(digit))):
        peer = peer_of(here, first, second, digit)
        source = tiles.at[pl.ds(peer * count, count)]
        copies.append(
            pltpu.make_async_copy(source, held.at[at * count : (at + 1) * count], sems.at[at])
        )
    return copies


def load_kernel(digit, steps, tiles, counts, node_block, slot_cell, *refs):
    *held, place, kept, sems, tile_sems = refs
    here = lax.axis_index("comp"), lax.axis_index("rank")
    copies = [
        pltpu.make_async_copy(source, target, sems.at[i])
        for i, (source, target) in enumerate(
            zip((counts, node_block, slot_cell), held, strict=True)
        )
    ]
    copies += tile_copies(digit, here, steps, tiles, kept, tile_sems)
    for copy in copies:
        copy.start()
    place[0], place[1] = here
    for copy in copies:
        copy.wait()


def choose_kernel(place, mine, other, fields):
    @pl.when(place[0] == 0)
    def _():
        fields[...] = mine[...]

    @pl.when(place[0] == 1)
    def _():
        fields[...] = other[...]


def forward_kernel(digit, steps, place, counts, node_block, fields, tiles, *messages):
    field_rows, width = fields.shape[0], tiles.shape[2]
    pair_slots = node_block.shape[0] // digit**2
    low = low_lanes((field_rows, width))
    own = low == (place[0] == 0)
    for index, (message, first) in enumerate(zip(messages, steps, strict=True)):
        for second in range(digit):
            peer = peer_of(place, first, second, digit)
            tile = (index * digit + second) * pair_slots
            live = counts[peer]
            rows = []
            for slot in range(0, pair_slots, 2):
                at = peer * pair_slots + slot
                sources = []
                for i in range(2):
                    columns = pl.ds(pl.multiple_of(node_block[at + i] * width, width), width)
                    sources.append(fields[:, columns])
                products = jnp.dot(
                    jnp.concatenate(sources, axis=0),
                    jnp.concatenate([tiles[tile + slot], tiles[tile + slot + 1]], axis=1),
                    preferred_element_type=jnp.float32,
                )
                even = jnp.where(slot < live, products[:field_rows, :width], 0.0)
                odd = jnp.where(slot + 1 < live, products[field_rows:, width:], 0.0)
                turned = half_turn(jnp.where(low, odd, even))
                rows.append(jnp.where(own, jnp.where(low, even, odd), turned))
            message[second] = jnp.concatenate(rows, axis=0).astype(message.dtype)


def own_kernel(digit, place, counts, node_block, fields, tiles, message, held, sems):
    copies = tile_copies(digit, (place[0], place[1]), [0], tiles, held, sems)
    for copy in copies:
        copy.start()
    for copy in copies:
        copy.wait()
    forward_kernel(digit, [0], place, counts, node_block, fields, held, message)


def repack_kernel(*refs):
    digit = (len(refs) + 1) // 2
    held, out = refs[:digit], refs[digit:]
    for index in range(1, digit):
        for first in range(digit):
            out[index - 1][first] = held[first][step_of(index, digit)]


def turn_kernel(place, tiles, out, held, sem):
    copy = pltpu.make_async_copy(tiles, held, sem)
    copy.start()
    rank_count, pairs, width, _ = out.shape
    mid = width // 2
    copy.wait()
    for d in range(rank_count):
        for pair in range(pairs):
            for i in range(2):
                turned = held[(d * pairs + pair) * 2 + i].T
                out[d, pair, i * mid : (i + 1) * mid] = jnp.where(
                    place[0] == 0, turned[:mid], turned[mid:]
                )


def add_entries(message, slot_cell, source, even_sums, odd_sums):
    field_rows = even_sums.shape[1]
    rows = message.astype(jnp.float32)
    for slot in range(0, slot_cell.shape[0], 2):
        entry = rows[slot // 2 * field_rows : (slot // 2 + 1) * field_rows]
        even_sums[slot_cell[slot, source]] += entry
        odd_sums[slot_cell[slot + 1, source]] += entry


def early_kernel(place, slot_cell, mine, other, *refs):
    *held, even_sums, odd_sums, surface = refs
    digit = len(held)
    nblocks, field_rows, width = surface.shape
    ocean_core = place[0] == 1
    own = low_lanes((field_rows, width)) != ocean_core
    even_sums[...] = jnp.zeros_like(even_sums)
    odd_sums[...] = jnp.zeros_like(odd_sums)
    for index in range(digit):
        source = peer_of(place, step_of(index, digit), 0, digit)
        add_entries(held[index][0], slot_cell, source, even_sums, odd_sums)
    for block in range(nblocks):
        columns = slice(block * width, (block + 1) * width)
        values = jnp.where(ocean_core, mine[:, columns], other[:, columns]).astype(jnp.float32)
        surface[block] = jnp.where(own, values, half_turn(values))


def middle_kernel(index, digit, place, slot_cell, arrived, _, __, even_sums, odd_sums):
    for first in range(digit):
        source = peer_of(place, step_of(first, digit), step_of(index, digit), digit)
        add_entries(arrived[first], slot_cell, source, even_sums, odd_sums)


def ocean_kernel(digit, place, slot_cell, surface, own_area, other_area, arrived, *refs):
    _, _, sending, flux, even_sums, odd_sums, near, far, pull = refs
    nblocks, field_rows, width = surface.shape
    flux_rows = field_rows // 2
    pair_slots, rank_count = slot_cell.shape
    ocean_core = place[0] == 1

    middle_kernel(digit - 1, digit, place, slot_cell, arrived, None, None, even_sums, odd_sums)

    low = low_lanes((field_rows, width))
    for block in range(nblocks):
        mixed = jnp.where(low, even_sums[block], odd_sums[block])
        remapped = mixed + half_turn(mixed)
        near[block] = remapped[:flux_rows] - surface[block, :flux_rows]
        far[block] = (remapped * surface[block])[flux_rows:]

    wind_u, wind_v, excess = near[:, 0, :], near[:, 1, :], near[:, 2, :]
    wind_speed = jnp.sqrt(wind_u * wind_u + wind_v * wind_v + 0.25)
    stability = 1.0 + 4.0 * jax.nn.sigmoid(excess)
    transfer = jnp.ones_like(wind_speed)
    for sweep in range(FLUX_IT):
        transfer = 1.0 / (1.0 + stability * transfer)
    pull[...] = transfer * wind_speed

    own = low_lanes((flux_rows, width)) != ocean_core
    own_rows = low_lanes((nblocks, width)) != ocean_core
    area = jnp.where(ocean_core, own_area[...], other_area[...])
    area = jnp.where(own_rows, area, half_turn(area))
    for block in range(nblocks):
        value = pull[block : block + 1] * near[block] + far[block]
        flux[:, block, :] = jnp.where(own, value, 0.0)
        far[block] = value * area[block : block + 1]

    low = low[:flux_rows]
    for source in range(rank_count):
        rows = []
        for slot in range(0, pair_slots, 2):
            even, odd = slot_cell[slot, source], slot_cell[slot + 1, source]
            rows.append(jnp.where(low, far[even], far[odd]))
        sending[source] = jnp.concatenate(rows, axis=0).astype(sending.dtype)


def back_kernel(core, place, counts, node_block, pieces, turned, flux, out, *sums):
    rank_count, pairs, width, _ = turned.shape
    flux_rows, nblocks, _ = flux.shape
    span = sums[0].shape[1]
    low = low_lanes((span, width))

    @pl.when(place[0] != core)
    def _():
        out[...] = flux[...]

    @pl.when(place[0] == core)
    def _():
        for total in sums:
            total[...] = jnp.zeros_like(total)
        for d in range(rank_count):
            live = counts[d]
            rows = pieces[d].astype(jnp.float32)
            for pair in range(pairs):
                start = pair * flux_rows // 8 * 8
                piece = rows[start : start + span]
                halves = [jnp.where(low, piece, 0.0), jnp.where(low, 0.0, piece)]
                products = jnp.dot(
                    jnp.concatenate(halves, axis=0).astype(jnp.bfloat16),
                    turned[d, pair],
                    preferred_element_type=jnp.float32,
                )
                total = sums[(pair * flux_rows - start) // 4]
                for i in range(2):
                    slot = 2 * pair + i
                    block = node_block[d * 2 * pairs + slot]
                    block = jnp.where(slot < live, block, nblocks)
                    total[block] += products[i * span : (i + 1) * span]
        for k in range(flux_rows):
            nodes = sums[0][:nblocks, k, :]
            for i, total in enumerate(sums[1:], 1):
                nodes += total[:nblocks, k + 4 * i, :]
            out[k] = nodes


def on_device(surface_fields, cell_area, remap_tiles, pair_blocks, slot_cell, node_block):
    rank_count = lax.axis_size("rank")
    digit = math.isqrt(rank_count)
    fields = surface_fields[0]
    width = remap_tiles.shape[1]
    pair_slots = slot_cell.shape[2]
    pairs = pair_slots // 2
    field_rows, points = fields.shape
    flux_rows = field_rows // 2
    nblocks = points // width
    by_block = (nblocks, width)
    core = lax.axis_index("comp")

    def in_vmem(value):
        return pltpu.with_memory_space_constraint(value, pltpu.VMEM)

    def in_hbm(value):
        return pltpu.with_memory_space_constraint(value, pltpu.HBM)

    def call(kernel, name, in_specs, out_shape, scratch_shapes=(), **options):
        return pl.pallas_call(
            kernel,
            in_specs=in_specs,
            out_specs=jax.tree.map(lambda out: pl.BlockSpec(memory_space=out.memory_space), out_shape),
            out_shape=out_shape,
            scratch_shapes=scratch_shapes,
            compiler_params=PARAMS,
            name=name,
            **options,
        )

    def to_peer(value, phase, step):
        jumps = (step, step * digit) if phase == 0 else (step * digit, step)
        pairs = [
            (part * rank_count + rank, part * rank_count + (rank ^ jump))
            for part, jump in enumerate(jumps)
            for rank in range(rank_count)
        ]
        return in_vmem(lax.ppermute(value, DEVICES, pairs))

    other_fields = swap_cores(fields)
    other_area = swap_cores(cell_area)

    other_fields, other_area = lax.optimization_barrier((other_fields, other_area))

    def part(steps):
        count = len(steps) * digit
        return [
            pltpu.VMEM((count * pair_slots, width, width), jnp.bfloat16),
            pltpu.SemaphoreType.DMA((count,)),
        ]

    steps = [step_of(i, digit) for i in range(1, digit)]
    operands = [remap_tiles, pair_blocks[0], node_block[0], slot_cell[0].T]
    loaded, load_sems = part(steps)
    *tables, tiles = call(
        functools.partial(load_kernel, digit, steps),
        "load_tiles",
        [ANY] * 4,
        [pltpu.SMEM(table.shape, jnp.int32) for table in operands[1:]]
        + [pltpu.SMEM((2,), jnp.int32), loaded],
        [pltpu.SemaphoreType.DMA((3,)), load_sems],
    )(*map(in_hbm, operands))
    counts, slot_nodes, cells, place = [
        pltpu.with_memory_space_constraint(table, pltpu.SMEM) for table in tables
    ]

    blocks = pltpu.VMEM((digit, pair_slots // 2 * field_rows, width), jnp.bfloat16)
    atmosphere = call(
        choose_kernel, "atmosphere", [SMEM, VMEM, VMEM], pltpu.VMEM(fields.shape, jnp.bfloat16)
    )(place, fields, other_fields)

    messages = call(
        functools.partial(forward_kernel, digit, steps),
        "forward_products",
        [SMEM, SMEM, SMEM, VMEM, VMEM],
        [blocks] * len(steps),
    )(place, counts, slot_nodes, atmosphere, tiles)
    at_home = call(
        functools.partial(own_kernel, digit),
        "own_products",
        [SMEM, SMEM, SMEM, VMEM, ANY],
        blocks,
        part([0]),
    )(place, counts, slot_nodes, atmosphere, in_hbm(remap_tiles))
    brought = [to_peer(value, 0, step) for value, step in zip(messages, steps, strict=True)]
    held = [at_home] + brought
    onward = call(repack_kernel, "repack", [VMEM] * digit, [blocks] * (digit - 1))(*held)
    arrived = [to_peer(onward[i - 1], 1, step_of(i, digit)) for i in range(1, digit)]

    sums = pltpu.VMEM((nblocks, field_rows, width), jnp.float32)
    even_sums, odd_sums, surface = call(
        early_kernel, "early_sums", [SMEM, SMEM] + [VMEM] * (2 + digit), [sums] * 3
    )(place, cells, fields, other_fields, *held)

    turned_tiles, surface = lax.optimization_barrier((remap_tiles, surface))
    turned = call(
        turn_kernel,
        "turn_tiles",
        [SMEM, ANY],
        pltpu.VMEM((rank_count, pairs, width, width), jnp.bfloat16),
        [pltpu.VMEM(remap_tiles.shape, jnp.bfloat16), pltpu.SemaphoreType.DMA],
    )(place, in_hbm(turned_tiles))
    turned, surface = lax.optimization_barrier((turned, surface))

    by_flux = pltpu.VMEM((flux_rows, nblocks, width), jnp.float32)
    rows = pltpu.VMEM((nblocks, flux_rows, width), jnp.float32)
    for i, value in enumerate(arrived[:-1]):
        even_sums, odd_sums = call(
            functools.partial(middle_kernel, i + 1, digit),
            "middle_sums",
            [SMEM, SMEM, VMEM, VMEM, VMEM],
            [sums, sums],
            input_output_aliases={3: 0, 4: 1},
        )(place, cells, value, even_sums, odd_sums)
    sending, ocean_flux, _, _ = call(
        functools.partial(ocean_kernel, digit),
        "ocean_fluxes",
        [SMEM, SMEM] + [VMEM] * 6,
        [
            pltpu.VMEM((rank_count, pairs * flux_rows, width), jnp.bfloat16),
            by_flux,
            sums,
            sums,
        ],
        [rows, rows, pltpu.VMEM(by_block, jnp.float32)],
        input_output_aliases={6: 2, 7: 3},
    )(
        place,
        cells,
        surface,
        cell_area.reshape(by_block),
        other_area.reshape(by_block),
        arrived[-1],
        even_sums,
        odd_sums,
    )
    returned = lax.all_to_all(sending, "rank", split_axis=0, concat_axis=0, tiled=True)

    span = -(-flux_rows // 8) * 8

    def back(core, name, returned):
        return call(
            functools.partial(back_kernel, core),
            name,
            [SMEM, SMEM, SMEM, VMEM, VMEM, VMEM],
            by_flux,
            [pltpu.VMEM((nblocks + 1, span, width), jnp.float32)] * 2,
        )(place, counts, slot_nodes, in_vmem(returned), turned, ocean_flux)

    give = back(1, "given_sums", returned)
    returned, give = lax.optimization_barrier((returned, give))
    keep = back(0, "kept_sums", returned)
    divisor = jnp.where(core == 1, 1.0, cell_area.reshape(by_block))
    return ((keep + swap_cores(give)) / divisor).reshape(1, flux_rows, points)


def solution(mesh):
    return jax.shard_map(
        on_device,
        mesh=mesh,
        in_specs=(
            P("comp", None, "rank"),
            P("comp", "rank"),
            P("rank", None, None),
            P("rank", None),
            P("rank", None, None),
            P("rank", None),
        ),
        out_specs=P("comp", None, "rank"),
        check_vma=False,
    )
```

```python
import functools
import itertools
import math

import jax
import jax.numpy as jnp
from jax import lax
from jax.experimental import pallas as pl
from jax.experimental.pallas import tpu as pltpu
from jax.sharding import PartitionSpec as P

FLUX_IT = 5
DEVICES = ("comp", "rank")
SMEM = pl.BlockSpec(memory_space=pltpu.SMEM)
VMEM = pl.BlockSpec(memory_space=pltpu.VMEM)
ANY = pl.BlockSpec(memory_space=pl.ANY)
PARAMS = pltpu.CompilerParams(vmem_limit_bytes=24 << 20)


def swap_cores(value):
    return lax.ppermute(value, "comp", [(0, 1), (1, 0)])


def low_lanes(shape):
    return lax.broadcasted_iota(jnp.int32, shape, len(shape) - 1) < shape[-1] // 2


def half_turn(value):
    return pltpu.roll(value, value.shape[-1] // 2, value.ndim - 1)


def step_of(index, digit):
    return digit - 1 if index == 1 else max(index - 1, 0)


def peer_of(place, first, second, digit):
    return place[1] ^ jnp.where(place[0] == 0, first + digit * second, digit * first + second)


def tile_copies(digit, here, steps, tiles, held, sems):
    count = tiles.shape[0] // digit**2
    copies = []
    for at, (first, second) in enumerate(itertools.product(steps, range(digit))):
        peer = peer_of(here, first, second, digit)
        source = tiles.at[pl.ds(peer * count, count)]
        copies.append(
            pltpu.make_async_copy(source, held.at[at * count : (at + 1) * count], sems.at[at])
        )
    return copies


def load_kernel(digit, steps, tiles, counts, node_block, slot_cell, *refs):
    *held, place, kept, sems, tile_sems = refs
    here = lax.axis_index("comp"), lax.axis_index("rank")
    copies = [
        pltpu.make_async_copy(source, target, sems.at[i])
        for i, (source, target) in enumerate(
            zip((counts, node_block, slot_cell), held, strict=True)
        )
    ]
    copies += tile_copies(digit, here, steps, tiles, kept, tile_sems)
    for copy in copies:
        copy.start()
    place[0], place[1] = here
    for copy in copies:
        copy.wait()


def choose_kernel(place, mine, other, fields):
    @pl.when(place[0] == 0)
    def _():
        fields[...] = mine[...]

    @pl.when(place[0] == 1)
    def _():
        fields[...] = other[...]


def forward_kernel(digit, steps, place, counts, node_block, fields, tiles, *messages):
    field_rows, width = fields.shape[0], tiles.shape[2]
    pair_slots = node_block.shape[0] // digit**2
    low = low_lanes((field_rows, width))
    own = low == (place[0] == 0)
    for index, (message, first) in enumerate(zip(messages, steps, strict=True)):
        for second in range(digit):
            peer = peer_of(place, first, second, digit)
            tile = (index * digit + second) * pair_slots
            live = counts[peer]
            rows = []
            for slot in range(0, pair_slots, 2):
                at = peer * pair_slots + slot
                sources = []
                for i in range(2):
                    columns = pl.ds(pl.multiple_of(node_block[at + i] * width, width), width)
                    sources.append(fields[:, columns])
                products = jnp.dot(
                    jnp.concatenate(sources, axis=0),
                    jnp.concatenate([tiles[tile + slot], tiles[tile + slot + 1]], axis=1),
                    preferred_element_type=jnp.float32,
                )
                even = jnp.where(slot < live, products[:field_rows, :width], 0.0)
                odd = jnp.where(slot + 1 < live, products[field_rows:, width:], 0.0)
                turned = half_turn(jnp.where(low, odd, even))
                rows.append(jnp.where(own, jnp.where(low, even, odd), turned))
            message[second] = jnp.concatenate(rows, axis=0).astype(message.dtype)


def own_kernel(digit, place, counts, node_block, fields, tiles, message, held, sems):
    copies = tile_copies(digit, (place[0], place[1]), [0], tiles, held, sems)
    for copy in copies:
        copy.start()
    for copy in copies:
        copy.wait()
    forward_kernel(digit, [0], place, counts, node_block, fields, held, message)


def repack_kernel(*refs):
    digit = (len(refs) + 1) // 2
    held, out = refs[:digit], refs[digit:]
    for index in range(1, digit):
        for first in range(digit):
            out[index - 1][first] = held[first][step_of(index, digit)]


def turn_kernel(place, tiles, out, held, sem):
    copy = pltpu.make_async_copy(tiles, held, sem)
    copy.start()
    rank_count, pairs, width, _ = out.shape
    mid = width // 2
    copy.wait()
    for d in range(rank_count):
        for pair in range(pairs):
            for i in range(2):
                turned = held[(d * pairs + pair) * 2 + i].T
                out[d, pair, i * mid : (i + 1) * mid] = jnp.where(
                    place[0] == 0, turned[:mid], turned[mid:]
                )


def add_entries(message, slot_cell, source, even_sums, odd_sums):
    field_rows = even_sums.shape[1]
    rows = message.astype(jnp.float32)
    for slot in range(0, slot_cell.shape[0], 2):
        entry = rows[slot // 2 * field_rows : (slot // 2 + 1) * field_rows]
        even_sums[slot_cell[slot, source]] += entry
        odd_sums[slot_cell[slot + 1, source]] += entry


def early_kernel(place, slot_cell, mine, other, *refs):
    *held, even_sums, odd_sums, surface = refs
    digit = len(held)
    nblocks, field_rows, width = surface.shape
    ocean_core = place[0] == 1
    own = low_lanes((field_rows, width)) != ocean_core
    even_sums[...] = jnp.zeros_like(even_sums)
    odd_sums[...] = jnp.zeros_like(odd_sums)
    for index in range(digit):
        source = peer_of(place, step_of(index, digit), 0, digit)
        add_entries(held[index][0], slot_cell, source, even_sums, odd_sums)
    for block in range(nblocks):
        columns = slice(block * width, (block + 1) * width)
        values = jnp.where(ocean_core, mine[:, columns], other[:, columns]).astype(jnp.float32)
        surface[block] = jnp.where(own, values, half_turn(values))


def middle_kernel(index, digit, place, slot_cell, arrived, _, __, even_sums, odd_sums):
    for first in range(digit):
        source = peer_of(place, step_of(first, digit), step_of(index, digit), digit)
        add_entries(arrived[first], slot_cell, source, even_sums, odd_sums)


def ocean_kernel(digit, place, slot_cell, surface, own_area, other_area, arrived, *refs):
    _, _, sending, flux, even_sums, odd_sums, near, far, pull = refs
    nblocks, field_rows, width = surface.shape
    flux_rows = field_rows // 2
    pair_slots, rank_count = slot_cell.shape
    ocean_core = place[0] == 1

    middle_kernel(digit - 1, digit, place, slot_cell, arrived, None, None, even_sums, odd_sums)

    low = low_lanes((field_rows, width))
    for block in range(nblocks):
        mixed = jnp.where(low, even_sums[block], odd_sums[block])
        remapped = mixed + half_turn(mixed)
        near[block] = remapped[:flux_rows] - surface[block, :flux_rows]
        far[block] = (remapped * surface[block])[flux_rows:]

    wind_u, wind_v, excess = near[:, 0, :], near[:, 1, :], near[:, 2, :]
    wind_speed = jnp.sqrt(wind_u * wind_u + wind_v * wind_v + 0.25)
    stability = 1.0 + 4.0 * jax.nn.sigmoid(excess)
    transfer = jnp.ones_like(wind_speed)
    for sweep in range(FLUX_IT):
        transfer = 1.0 / (1.0 + stability * transfer)
    pull[...] = transfer * wind_speed

    own = low_lanes((flux_rows, width)) != ocean_core
    own_rows = low_lanes((nblocks, width)) != ocean_core
    area = jnp.where(ocean_core, own_area[...], other_area[...])
    area = jnp.where(own_rows, area, half_turn(area))
    for block in range(nblocks):
        value = pull[block : block + 1] * near[block] + far[block]
        flux[:, block, :] = jnp.where(own, value, 0.0)
        far[block] = value * area[block : block + 1]

    low = low[:flux_rows]
    for source in range(rank_count):
        rows = []
        for slot in range(0, pair_slots, 2):
            even, odd = slot_cell[slot, source], slot_cell[slot + 1, source]
            rows.append(jnp.where(low, far[even], far[odd]))
        sending[source] = jnp.concatenate(rows, axis=0).astype(sending.dtype)


def back_kernel(core, place, counts, node_block, pieces, turned, flux, out, *sums):
    rank_count, pairs, width, _ = turned.shape
    flux_rows, nblocks, _ = flux.shape
    span = sums[0].shape[1]
    low = low_lanes((span, width))

    @pl.when(place[0] != core)
    def _():
        out[...] = flux[...].astype(out.dtype)

    @pl.when(place[0] == core)
    def _():
        for total in sums:
            total[...] = jnp.zeros_like(total)
        for d in range(rank_count):
            live = counts[d]
            rows = pieces[d].astype(jnp.float32)
            for pair in range(pairs):
                start = pair * flux_rows // 8 * 8
                piece = rows[start : start + span]
                halves = [jnp.where(low, piece, 0.0), jnp.where(low, 0.0, piece)]
                products = jnp.dot(
                    jnp.concatenate(halves, axis=0).astype(jnp.bfloat16),
                    turned[d, pair],
                    preferred_element_type=jnp.float32,
                )
                total = sums[(pair * flux_rows - start) // 4]
                for i in range(2):
                    slot = 2 * pair + i
                    block = node_block[d * 2 * pairs + slot]
                    block = jnp.where(slot < live, block, nblocks)
                    total[block] += products[i * span : (i + 1) * span]
        for k in range(flux_rows):
            nodes = sums[0][:nblocks, k, :]
            for i, total in enumerate(sums[1:], 1):
                nodes += total[:nblocks, k + 4 * i, :]
            out[k] = nodes.astype(out.dtype)


def on_device(surface_fields, cell_area, remap_tiles, pair_blocks, slot_cell, node_block):
    rank_count = lax.axis_size("rank")
    digit = math.isqrt(rank_count)
    fields = surface_fields[0]
    width = remap_tiles.shape[1]
    pair_slots = slot_cell.shape[2]
    pairs = pair_slots // 2
    field_rows, points = fields.shape
    flux_rows = field_rows // 2
    nblocks = points // width
    by_block = (nblocks, width)
    core = lax.axis_index("comp")

    def in_vmem(value):
        return pltpu.with_memory_space_constraint(value, pltpu.VMEM)

    def in_hbm(value):
        return pltpu.with_memory_space_constraint(value, pltpu.HBM)

    def call(kernel, name, in_specs, out_shape, scratch_shapes=(), **options):
        return pl.pallas_call(
            kernel,
            in_specs=in_specs,
            out_specs=jax.tree.map(lambda out: pl.BlockSpec(memory_space=out.memory_space), out_shape),
            out_shape=out_shape,
            scratch_shapes=scratch_shapes,
            compiler_params=PARAMS,
            name=name,
            **options,
        )

    def to_peer(value, phase, step):
        jumps = (step, step * digit) if phase == 0 else (step * digit, step)
        pairs = [
            (part * rank_count + rank, part * rank_count + (rank ^ jump))
            for part, jump in enumerate(jumps)
            for rank in range(rank_count)
        ]
        return in_vmem(lax.ppermute(value, DEVICES, pairs))

    other_fields = swap_cores(fields)
    other_area = swap_cores(cell_area)

    other_fields, other_area = lax.optimization_barrier((other_fields, other_area))

    def part(steps):
        count = len(steps) * digit
        return [
            pltpu.VMEM((count * pair_slots, width, width), jnp.bfloat16),
            pltpu.SemaphoreType.DMA((count,)),
        ]

    steps = [step_of(i, digit) for i in range(1, digit)]
    operands = [remap_tiles, pair_blocks[0], node_block[0], slot_cell[0].T]
    loaded, load_sems = part(steps)
    *tables, tiles = call(
        functools.partial(load_kernel, digit, steps),
        "load_tiles",
        [ANY] * 4,
        [pltpu.SMEM(table.shape, jnp.int32) for table in operands[1:]]
        + [pltpu.SMEM((2,), jnp.int32), loaded],
        [pltpu.SemaphoreType.DMA((3,)), load_sems],
    )(*map(in_hbm, operands))
    counts, slot_nodes, cells, place = [
        pltpu.with_memory_space_constraint(table, pltpu.SMEM) for table in tables
    ]

    blocks = pltpu.VMEM((digit, pair_slots // 2 * field_rows, width), jnp.bfloat16)
    atmosphere = call(
        choose_kernel, "atmosphere", [SMEM, VMEM, VMEM], pltpu.VMEM(fields.shape, jnp.bfloat16)
    )(place, fields, other_fields)

    messages = call(
        functools.partial(forward_kernel, digit, steps),
        "forward_products",
        [SMEM, SMEM, SMEM, VMEM, VMEM],
        [blocks] * len(steps),
    )(place, counts, slot_nodes, atmosphere, tiles)
    at_home = call(
        functools.partial(own_kernel, digit),
        "own_products",
        [SMEM, SMEM, SMEM, VMEM, ANY],
        blocks,
        part([0]),
    )(place, counts, slot_nodes, atmosphere, in_hbm(remap_tiles))
    brought = [to_peer(value, 0, step) for value, step in zip(messages, steps, strict=True)]
    held = [at_home] + brought
    onward = call(repack_kernel, "repack", [VMEM] * digit, [blocks] * (digit - 1))(*held)
    arrived = [to_peer(onward[i - 1], 1, step_of(i, digit)) for i in range(1, digit)]

    sums = pltpu.VMEM((nblocks, field_rows, width), jnp.float32)
    even_sums, odd_sums, surface = call(
        early_kernel, "early_sums", [SMEM, SMEM] + [VMEM] * (2 + digit), [sums] * 3
    )(place, cells, fields, other_fields, *held)

    turned_tiles, surface = lax.optimization_barrier((remap_tiles, surface))
    turned = call(
        turn_kernel,
        "turn_tiles",
        [SMEM, ANY],
        pltpu.VMEM((rank_count, pairs, width, width), jnp.bfloat16),
        [pltpu.VMEM(remap_tiles.shape, jnp.bfloat16), pltpu.SemaphoreType.DMA],
    )(place, in_hbm(turned_tiles))
    turned, surface = lax.optimization_barrier((turned, surface))

    by_flux = pltpu.VMEM((flux_rows, nblocks, width), jnp.float32)
    rows = pltpu.VMEM((nblocks, flux_rows, width), jnp.float32)
    for i, value in enumerate(arrived[:-1]):
        even_sums, odd_sums = call(
            functools.partial(middle_kernel, i + 1, digit),
            "middle_sums",
            [SMEM, SMEM, VMEM, VMEM, VMEM],
            [sums, sums],
            input_output_aliases={3: 0, 4: 1},
        )(place, cells, value, even_sums, odd_sums)
    sending, ocean_flux, _, _ = call(
        functools.partial(ocean_kernel, digit),
        "ocean_fluxes",
        [SMEM, SMEM] + [VMEM] * 6,
        [
            pltpu.VMEM((rank_count, pairs * flux_rows, width), jnp.bfloat16),
            by_flux,
            sums,
            sums,
        ],
        [rows, rows, pltpu.VMEM(by_block, jnp.float32)],
        input_output_aliases={6: 2, 7: 3},
    )(
        place,
        cells,
        surface,
        cell_area.reshape(by_block),
        other_area.reshape(by_block),
        arrived[-1],
        even_sums,
        odd_sums,
    )
    returned = lax.all_to_all(sending, "rank", split_axis=0, concat_axis=0, tiled=True)

    span = -(-flux_rows // 8) * 8

    def back(core, name, returned, out):
        return call(
            functools.partial(back_kernel, core),
            name,
            [SMEM, SMEM, SMEM, VMEM, VMEM, VMEM],
            pltpu.VMEM(by_flux.shape, out),
            [pltpu.VMEM((nblocks + 1, span, width), jnp.float32)] * 2,
        )(place, counts, slot_nodes, in_vmem(returned), turned, ocean_flux)

    give = back(1, "given_sums", returned, jnp.bfloat16)
    returned, give = lax.optimization_barrier((returned, give))
    keep = back(0, "kept_sums", returned, jnp.float32)
    divisor = jnp.where(core == 1, 1.0, cell_area.reshape(by_block))
    return ((keep + swap_cores(give).astype(jnp.float32)) / divisor).reshape(1, flux_rows, points)


def solution(mesh):
    return jax.shard_map(
        on_device,
        mesh=mesh,
        in_specs=(
            P("comp", None, "rank"),
            P("comp", "rank"),
            P("rank", None, None),
            P("rank", None),
            P("rank", None, None),
            P("rank", None),
        ),
        out_specs=P("comp", None, "rank"),
        check_vma=False,
    )
```

```python
import functools
import itertools
import math

import jax
import jax.numpy as jnp
from jax import lax
from jax.experimental import pallas as pl
from jax.experimental.pallas import tpu as pltpu
from jax.sharding import PartitionSpec as P

FLUX_IT = 5
DEVICES = ("comp", "rank")
SMEM = pl.BlockSpec(memory_space=pltpu.SMEM)
VMEM = pl.BlockSpec(memory_space=pltpu.VMEM)
ANY = pl.BlockSpec(memory_space=pl.ANY)
PARAMS = pltpu.CompilerParams(vmem_limit_bytes=24 << 20)


def swap_cores(value):
    return lax.ppermute(value, "comp", [(0, 1), (1, 0)])


def low_lanes(shape):
    return lax.broadcasted_iota(jnp.int32, shape, len(shape) - 1) < shape[-1] // 2


def half_turn(value):
    return pltpu.roll(value, value.shape[-1] // 2, value.ndim - 1)


def step_of(index, digit):
    return digit - 1 if index == 1 else max(index - 1, 0)


def peer_of(place, first, second, digit):
    return place[1] ^ jnp.where(place[0] == 0, first + digit * second, digit * first + second)


def tile_copies(digit, here, steps, tiles, held, sems):
    count = tiles.shape[0] // digit**2
    copies = []
    for at, (first, second) in enumerate(itertools.product(steps, range(digit))):
        peer = peer_of(here, first, second, digit)
        source = tiles.at[pl.ds(peer * count, count)]
        copies.append(
            pltpu.make_async_copy(source, held.at[at * count : (at + 1) * count], sems.at[at])
        )
    return copies


def load_kernel(digit, steps, tiles, counts, node_block, slot_cell, *refs):
    *held, place, kept, sems, tile_sems = refs
    here = lax.axis_index("comp"), lax.axis_index("rank")
    copies = [
        pltpu.make_async_copy(source, target, sems.at[i])
        for i, (source, target) in enumerate(
            zip((counts, node_block, slot_cell), held, strict=True)
        )
    ]
    copies = tile_copies(digit, here, steps, tiles, kept, tile_sems) + copies
    for copy in copies:
        copy.start()
    place[0], place[1] = here
    for copy in copies:
        copy.wait()


def choose_kernel(place, mine, other, fields):
    @pl.when(place[0] == 0)
    def _():
        fields[...] = mine[...]

    @pl.when(place[0] == 1)
    def _():
        fields[...] = other[...]


def forward_kernel(digit, steps, place, counts, node_block, fields, tiles, *messages):
    field_rows, width = fields.shape[0], tiles.shape[2]
    pair_slots = node_block.shape[0] // digit**2
    low = low_lanes((field_rows, width))
    own = low == (place[0] == 0)
    for index, (message, first) in enumerate(zip(messages, steps, strict=True)):
        for second in range(digit):
            peer = peer_of(place, first, second, digit)
            tile = (index * digit + second) * pair_slots
            live = counts[peer]
            rows = []
            for slot in range(0, pair_slots, 2):
                at = peer * pair_slots + slot
                sources = []
                for i in range(2):
                    columns = pl.ds(pl.multiple_of(node_block[at + i] * width, width), width)
                    sources.append(fields[:, columns])
                products = jnp.dot(
                    jnp.concatenate(sources, axis=0),
                    jnp.concatenate([tiles[tile + slot], tiles[tile + slot + 1]], axis=1),
                    preferred_element_type=jnp.float32,
                )
                even = jnp.where(slot < live, products[:field_rows, :width], 0.0)
                odd = jnp.where(slot + 1 < live, products[field_rows:, width:], 0.0)
                turned = half_turn(jnp.where(low, odd, even))
                rows.append(jnp.where(own, jnp.where(low, even, odd), turned))
            message[second] = jnp.concatenate(rows, axis=0).astype(message.dtype)


def own_kernel(digit, place, counts, node_block, fields, tiles, message, held, sems):
    copies = tile_copies(digit, (place[0], place[1]), [0], tiles, held, sems)
    for copy in copies:
        copy.start()
    for copy in copies:
        copy.wait()
    forward_kernel(digit, [0], place, counts, node_block, fields, held, message)


def repack_kernel(*refs):
    digit = (len(refs) + 1) // 2
    held, out = refs[:digit], refs[digit:]
    for index in range(1, digit):
        for first in range(digit):
            out[index - 1][first] = held[first][step_of(index, digit)]


def turn_kernel(place, tiles, out, held, sem):
    copy = pltpu.make_async_copy(tiles, held, sem)
    copy.start()
    rank_count, pairs, width, _ = out.shape
    mid = width // 2
    copy.wait()
    for d in range(rank_count):
        for pair in range(pairs):
            for i in range(2):
                turned = held[(d * pairs + pair) * 2 + i].T
                out[d, pair, i * mid : (i + 1) * mid] = jnp.where(
                    place[0] == 0, turned[:mid], turned[mid:]
                )


def add_entries(message, slot_cell, source, even_sums, odd_sums):
    field_rows = even_sums.shape[1]
    rows = message.astype(jnp.float32)
    for slot in range(0, slot_cell.shape[0], 2):
        entry = rows[slot // 2 * field_rows : (slot // 2 + 1) * field_rows]
        even_sums[slot_cell[slot, source]] += entry
        odd_sums[slot_cell[slot + 1, source]] += entry


def early_kernel(place, slot_cell, mine, other, *refs):
    *held, even_sums, odd_sums, surface = refs
    digit = len(held)
    nblocks, field_rows, width = surface.shape
    ocean_core = place[0] == 1
    own = low_lanes((field_rows, width)) != ocean_core
    even_sums[...] = jnp.zeros_like(even_sums)
    odd_sums[...] = jnp.zeros_like(odd_sums)
    for index in range(digit):
        source = peer_of(place, step_of(index, digit), 0, digit)
        add_entries(held[index][0], slot_cell, source, even_sums, odd_sums)
    for block in range(nblocks):
        columns = slice(block * width, (block + 1) * width)
        values = jnp.where(ocean_core, mine[:, columns], other[:, columns]).astype(jnp.float32)
        surface[block] = jnp.where(own, values, half_turn(values))


def middle_kernel(index, digit, place, slot_cell, arrived, _, __, even_sums, odd_sums):
    for first in range(digit):
        source = peer_of(place, step_of(first, digit), step_of(index, digit), digit)
        add_entries(arrived[first], slot_cell, source, even_sums, odd_sums)


def ocean_kernel(digit, place, slot_cell, surface, own_area, other_area, arrived, *refs):
    _, _, sending, flux, even_sums, odd_sums, near, far, pull = refs
    nblocks, field_rows, width = surface.shape
    flux_rows = field_rows // 2
    pair_slots, rank_count = slot_cell.shape
    ocean_core = place[0] == 1

    middle_kernel(digit - 1, digit, place, slot_cell, arrived, None, None, even_sums, odd_sums)

    low = low_lanes((field_rows, width))
    for block in range(nblocks):
        mixed = jnp.where(low, even_sums[block], odd_sums[block])
        remapped = mixed + half_turn(mixed)
        near[block] = remapped[:flux_rows] - surface[block, :flux_rows]
        far[block] = (remapped * surface[block])[flux_rows:]

    wind_u, wind_v, excess = near[:, 0, :], near[:, 1, :], near[:, 2, :]
    wind_speed = jnp.sqrt(wind_u * wind_u + wind_v * wind_v + 0.25)
    stability = 1.0 + 4.0 * jax.nn.sigmoid(excess)
    transfer = jnp.ones_like(wind_speed)
    for sweep in range(FLUX_IT):
        transfer = 1.0 / (1.0 + stability * transfer)
    pull[...] = transfer * wind_speed

    own = low_lanes((flux_rows, width)) != ocean_core
    own_rows = low_lanes((nblocks, width)) != ocean_core
    area = jnp.where(ocean_core, own_area[...], other_area[...])
    area = jnp.where(own_rows, area, half_turn(area))
    for block in range(nblocks):
        value = pull[block : block + 1] * near[block] + far[block]
        flux[:, block, :] = jnp.where(own, value, 0.0)
        far[block] = value * area[block : block + 1]

    low = low[:flux_rows]
    for source in range(rank_count):
        rows = []
        for slot in range(0, pair_slots, 2):
            even, odd = slot_cell[slot, source], slot_cell[slot + 1, source]
            rows.append(jnp.where(low, far[even], far[odd]))
        sending[source] = jnp.concatenate(rows, axis=0).astype(sending.dtype)


def back_kernel(core, place, counts, node_block, pieces, turned, flux, out, *sums):
    rank_count, pairs, width, _ = turned.shape
    flux_rows, nblocks, _ = flux.shape
    span = sums[0].shape[1]
    low = low_lanes((span, width))

    @pl.when(place[0] != core)
    def _():
        out[...] = flux[...]

    @pl.when(place[0] == core)
    def _():
        for total in sums:
            total[...] = jnp.zeros_like(total)
        for d in range(rank_count):
            live = counts[d]
            rows = pieces[d].astype(jnp.float32)
            for pair in range(pairs):
                start = pair * flux_rows // 8 * 8
                piece = rows[start : start + span]
                halves = [jnp.where(low, piece, 0.0), jnp.where(low, 0.0, piece)]
                products = jnp.dot(
                    jnp.concatenate(halves, axis=0).astype(jnp.bfloat16),
                    turned[d, pair],
                    preferred_element_type=jnp.float32,
                )
                total = sums[(pair * flux_rows - start) // 4]
                for i in range(2):
                    slot = 2 * pair + i
                    block = node_block[d * 2 * pairs + slot]
                    block = jnp.where(slot < live, block, nblocks)
                    total[block] += products[i * span : (i + 1) * span]
        for k in range(flux_rows):
            nodes = sums[0][:nblocks, k, :]
            for i, total in enumerate(sums[1:], 1):
                nodes += total[:nblocks, k + 4 * i, :]
            out[k] = nodes


def on_device(surface_fields, cell_area, remap_tiles, pair_blocks, slot_cell, node_block):
    rank_count = lax.axis_size("rank")
    digit = math.isqrt(rank_count)
    fields = surface_fields[0]
    width = remap_tiles.shape[1]
    pair_slots = slot_cell.shape[2]
    pairs = pair_slots // 2
    field_rows, points = fields.shape
    flux_rows = field_rows // 2
    nblocks = points // width
    by_block = (nblocks, width)
    core = lax.axis_index("comp")

    def in_vmem(value):
        return pltpu.with_memory_space_constraint(value, pltpu.VMEM)

    def in_hbm(value):
        return pltpu.with_memory_space_constraint(value, pltpu.HBM)

    def call(kernel, name, in_specs, out_shape, scratch_shapes=(), **options):
        return pl.pallas_call(
            kernel,
            in_specs=in_specs,
            out_specs=jax.tree.map(lambda out: pl.BlockSpec(memory_space=out.memory_space), out_shape),
            out_shape=out_shape,
            scratch_shapes=scratch_shapes,
            compiler_params=PARAMS,
            name=name,
            **options,
        )

    def to_peer(value, phase, step):
        jumps = (step, step * digit) if phase == 0 else (step * digit, step)
        pairs = [
            (part * rank_count + rank, part * rank_count + (rank ^ jump))
            for part, jump in enumerate(jumps)
            for rank in range(rank_count)
        ]
        return in_vmem(lax.ppermute(value, DEVICES, pairs))

    other_fields = swap_cores(fields)
    other_area = swap_cores(cell_area)

    other_fields, other_area = lax.optimization_barrier((other_fields, other_area))

    def part(steps):
        count = len(steps) * digit
        return [
            pltpu.VMEM((count * pair_slots, width, width), jnp.bfloat16),
            pltpu.SemaphoreType.DMA((count,)),
        ]

    steps = [step_of(i, digit) for i in range(1, digit)]
    operands = [remap_tiles, pair_blocks[0], node_block[0], slot_cell[0].T]
    loaded, load_sems = part(steps)
    *tables, tiles = call(
        functools.partial(load_kernel, digit, steps),
        "load_tiles",
        [ANY] * 4,
        [pltpu.SMEM(table.shape, jnp.int32) for table in operands[1:]]
        + [pltpu.SMEM((2,), jnp.int32), loaded],
        [pltpu.SemaphoreType.DMA((3,)), load_sems],
    )(*map(in_hbm, operands))
    counts, slot_nodes, cells, place = [
        pltpu.with_memory_space_constraint(table, pltpu.SMEM) for table in tables
    ]

    blocks = pltpu.VMEM((digit, pair_slots // 2 * field_rows, width), jnp.bfloat16)
    atmosphere = call(
        choose_kernel, "atmosphere", [SMEM, VMEM, VMEM], pltpu.VMEM(fields.shape, jnp.bfloat16)
    )(place, fields, other_fields)

    messages = call(
        functools.partial(forward_kernel, digit, steps),
        "forward_products",
        [SMEM, SMEM, SMEM, VMEM, VMEM],
        [blocks] * len(steps),
    )(place, counts, slot_nodes, atmosphere, tiles)
    at_home = call(
        functools.partial(own_kernel, digit),
        "own_products",
        [SMEM, SMEM, SMEM, VMEM, ANY],
        blocks,
        part([0]),
    )(place, counts, slot_nodes, atmosphere, in_hbm(remap_tiles))
    brought = [to_peer(value, 0, step) for value, step in zip(messages, steps, strict=True)]
    held = [at_home] + brought
    onward = call(repack_kernel, "repack", [VMEM] * digit, [blocks] * (digit - 1))(*held)
    arrived = [to_peer(onward[i - 1], 1, step_of(i, digit)) for i in range(1, digit)]

    sums = pltpu.VMEM((nblocks, field_rows, width), jnp.float32)
    even_sums, odd_sums, surface = call(
        early_kernel, "early_sums", [SMEM, SMEM] + [VMEM] * (2 + digit), [sums] * 3
    )(place, cells, fields, other_fields, *held)

    turned_tiles, surface = lax.optimization_barrier((remap_tiles, surface))
    turned = call(
        turn_kernel,
        "turn_tiles",
        [SMEM, ANY],
        pltpu.VMEM((rank_count, pairs, width, width), jnp.bfloat16),
        [pltpu.VMEM(remap_tiles.shape, jnp.bfloat16), pltpu.SemaphoreType.DMA],
    )(place, in_hbm(turned_tiles))
    turned, surface = lax.optimization_barrier((turned, surface))

    by_flux = pltpu.VMEM((flux_rows, nblocks, width), jnp.float32)
    rows = pltpu.VMEM((nblocks, flux_rows, width), jnp.float32)
    for i, value in enumerate(arrived[:-1]):
        even_sums, odd_sums = call(
            functools.partial(middle_kernel, i + 1, digit),
            "middle_sums",
            [SMEM, SMEM, VMEM, VMEM, VMEM],
            [sums, sums],
            input_output_aliases={3: 0, 4: 1},
        )(place, cells, value, even_sums, odd_sums)
    sending, ocean_flux, _, _ = call(
        functools.partial(ocean_kernel, digit),
        "ocean_fluxes",
        [SMEM, SMEM] + [VMEM] * 6,
        [
            pltpu.VMEM((rank_count, pairs * flux_rows, width), jnp.bfloat16),
            by_flux,
            sums,
            sums,
        ],
        [rows, rows, pltpu.VMEM(by_block, jnp.float32)],
        input_output_aliases={6: 2, 7: 3},
    )(
        place,
        cells,
        surface,
        cell_area.reshape(by_block),
        other_area.reshape(by_block),
        arrived[-1],
        even_sums,
        odd_sums,
    )
    returned = lax.all_to_all(sending, "rank", split_axis=0, concat_axis=0, tiled=True)

    span = -(-flux_rows // 8) * 8

    def back(core, name, returned):
        return call(
            functools.partial(back_kernel, core),
            name,
            [SMEM, SMEM, SMEM, VMEM, VMEM, VMEM],
            by_flux,
            [pltpu.VMEM((nblocks + 1, span, width), jnp.float32)] * 2,
        )(place, counts, slot_nodes, in_vmem(returned), turned, ocean_flux)

    give = back(1, "given_sums", returned)
    returned, give = lax.optimization_barrier((returned, give))
    keep = back(0, "kept_sums", returned)
    divisor = jnp.where(core == 1, 1.0, cell_area.reshape(by_block))
    return ((keep + swap_cores(give)) / divisor).reshape(1, flux_rows, points)


def solution(mesh):
    return jax.shard_map(
        on_device,
        mesh=mesh,
        in_specs=(
            P("comp", None, "rank"),
            P("comp", "rank"),
            P("rank", None, None),
            P("rank", None),
            P("rank", None, None),
            P("rank", None),
        ),
        out_specs=P("comp", None, "rank"),
        check_vma=False,
    )
```
